256 devices in a mesh: box: 64 (over z, y, core), grp: 4 (over x).
Axes of the slice: x: 4, y: 4, z: 8, core: 2. Of those that a mesh axis runs over, the one named last changes fastest.
Arguments:
- exp_fine: bfloat16 [65536, 512], P('box'), may hold values from -6 to 6
- req_fine: int32 [4096, 128], P('box'), may hold values from -1 to 1023, as said below
- src_fine: int32 [2048, 1024], P(('box', 'grp')), may hold values from -1 to 9215, as said below
- exp_coarse: bfloat16 [8192, 512], P('box'), may hold values from -6 to 6
- req_coarse: int32 [4096, 32], P('box'), may hold values from -1 to 127, as said below
- src_coarse: int32 [2048, 128], P(('box', 'grp')), may hold values from -1 to 2175, as said below
- operators: bfloat16 [32, 512, 512], P('grp'), may hold values from -0.03125 to 0.03125
- l2l_ops: bfloat16 [8, 512, 512], replicated, may hold values from -0.25 to 0.25
- relay_src: int32 [65536], P('box'), may hold values from 0 to 65535, as said below
Outputs:
- local_field: bfloat16 [65536, 512], P('box')
The draws below stay inside these ranges and needn't reach their ends.
Inputs may be any that keep to these rules, and one draw needn't show every extreme that they name: `req_fine`: -1 marks an empty slot. `req_coarse`: -1 marks an empty slot. `src_fine`: -1 marks a target box that the operator does not reach; in every block of 32 rows the first row has no -1. `src_coarse`: -1 marks a target box that the operator does not reach; in every block of 32 rows the first row has no -1. A permutation; relay_src[i] lies in the block of 1024 rows that holds i or within 32 rows of it in a neighbouring block.
All inputs are finite; a program needn't handle non-finite values.
Results may differ from the reference program's by a relative error of at most 0.0049.
Values may be sent and summed in bfloat16 or wider, within the bound.
No kernel may reach another device: no remote copies, remote signals or barrier semaphores. Data moves between devices by JAX's collectives and lax.ppermute only.
A program may use at most 128 MiB of HBM per device.

```python
import jax
import jax.numpy as jnp
from jax import lax

P_SIZE = 512
BF = 1024
R = 32
BC = 128
C_F = 128
C_C = 32
K_F = 1024
K_C = 128
OPS = 32
BOXES_F = 65536
BOXES_C = 8192
SRC_F = 9216
SRC_C = 2176
N_BOX = 64


def request_table(key, block_rows, slot_count):
    key_rows, key_keep = jax.random.split(key)
    shape = (N_BOX * N_BOX, slot_count)
    chosen = jax.random.randint(key_rows, shape, 0, block_rows, dtype=jnp.int32)
    filled = jax.random.randint(key_keep, shape, 0, 3, dtype=jnp.int32) > 0
    table = jnp.where(filled, chosen, -1)
    table = table.at[0, 0].set(block_rows - 1)
    table = table.at[0, 1].set(-1)
    return table.astype(jnp.int32)


def pair_sources(key, span, slot_count):
    key_count, key_rows, key_keep = jax.random.split(key, 3)
    row_total = N_BOX * OPS
    filled_count = jax.random.randint(key_count, (row_total, 1), slot_count // 4, slot_count + 1, dtype=jnp.int32)
    row_index = jnp.arange(row_total, dtype=jnp.int32)[:, None]
    filled_count = jnp.where(row_index % OPS == 0, slot_count, filled_count)
    filled_count = jnp.where(row_index == 1, slot_count // 4, filled_count)
    chosen = jax.random.randint(key_rows, (row_total, slot_count), 0, span, dtype=jnp.int32)
    ticket = jax.random.randint(key_keep, (row_total, slot_count), 0, slot_count, dtype=jnp.int32)
    keep = (ticket < filled_count) | (row_index % OPS == 0)
    result = jnp.where(keep, chosen, -1)
    result = result.at[0, 0].set(span - 1)
    result = result.at[1, 0].set(-1)
    return result.astype(jnp.int32)


def draw_req_fine(key, part):
    key = jax.random.fold_in(key, 1)
    return request_table(key, BF, C_F)


def draw_req_coarse(key, part):
    key = jax.random.fold_in(key, 2)
    return request_table(key, BC, C_C)


def draw_src_fine(key, part):
    key = jax.random.fold_in(key, 3)
    return pair_sources(key, SRC_F, K_F)


def draw_src_coarse(key, part):
    key = jax.random.fold_in(key, 4)
    return pair_sources(key, SRC_C, K_C)


def draw_relay_src(key, part):
    key = jax.random.fold_in(key, 5)
    shifts = jax.random.randint(key, (N_BOX,), 1, R + 1, dtype=jnp.int32)
    shifts = shifts.at[0].set(R)
    shifts = shifts.at[N_BOX - 1].set(0)
    row_index = jnp.arange(N_BOX * BF, dtype=jnp.int32)
    block_index = row_index // BF
    position = row_index % BF
    right_count = shifts[block_index]
    left_count = jnp.where(block_index > 0, shifts[jnp.clip(block_index - 1, 0, None)], 0)
    from_right = (block_index + 1) * BF + position - (BF - right_count)
    from_left = (block_index - 1) * BF + BF - left_count + position
    result = jnp.where(position >= BF - right_count, from_right, jnp.where(position < left_count, from_left, row_index))
    return result.astype(jnp.int32)


def level_of(key, extent, shards, smallest, high):
    loudness = 1.0
    for dim, shards_of in shards:
        heights = jax.random.uniform(jax.random.fold_in(jax.random.fold_in(key, 6), dim), (shards_of,), jnp.float32, smallest / len(shards), high / len(shards))
        loudness = loudness * jnp.repeat(jnp.exp(heights), extent[dim] // shards_of).reshape((-1,) + (1,) * (len(extent) - 1 - dim))
    return loudness


def normal_values(own_key, extent, scale, most, cuts=(), kind=jnp.bfloat16):
    entries = jax.random.normal(own_key, extent, jnp.float32) * scale
    if len(cuts) > 0:
        entries = level_of(own_key, extent, cuts, -0.22, 0.18) * entries
    return jnp.clip(entries, min=-most, max=most).astype(kind)


def setup_inputs(seed: int = 0) -> dict:
    key_list = jax.random.split(jax.random.key(seed), 10)
    exp_fine = normal_values(key_list[0], (BOXES_F, P_SIZE), 1.0, 6.0, ((0, 64),))
    req_fine = draw_req_fine(jax.random.fold_in(key_list[9], 71), 0)
    src_fine = draw_src_fine(jax.random.fold_in(key_list[9], 71), 0)
    exp_coarse = normal_values(key_list[3], (BOXES_C, P_SIZE), 1.0, 6.0, ((0, 64),))
    req_coarse = draw_req_coarse(jax.random.fold_in(key_list[9], 71), 0)
    src_coarse = draw_src_coarse(jax.random.fold_in(key_list[9], 71), 0)
    operators = normal_values(key_list[6], (OPS, P_SIZE, P_SIZE), (P_SIZE * 64) ** -0.5, 0.03125, ((0, 4),))
    l2l_ops = normal_values(key_list[7], (8, P_SIZE, P_SIZE), P_SIZE ** -0.5, 0.25)
    relay_src = draw_relay_src(jax.random.fold_in(key_list[9], 71), 0)
    return {"exp_fine": exp_fine, "req_fine": req_fine, "src_fine": src_fine, "exp_coarse": exp_coarse, "req_coarse": req_coarse, "src_coarse": src_coarse, "operators": operators, "l2l_ops": l2l_ops, "relay_src": relay_src}


def far_level(expansions, requests, sources, operators, block_rows, level_factor):
    coefficients = expansions.shape[1]
    op_count = operators.shape[0]
    op_float = operators.astype(jnp.float32)

    def one_block(device):
        own_rows = lax.dynamic_slice_in_dim(expansions, device * block_rows, block_rows, 0)
        wanted = lax.dynamic_slice_in_dim(requests, device * N_BOX, N_BOX, 0)
        global_rows = jnp.arange(N_BOX, dtype=jnp.int32)[:, None] * block_rows + jnp.clip(wanted, 0, None)
        remote = jnp.where((wanted >= 0)[:, :, None], expansions[global_rows], jnp.zeros((), jnp.bfloat16))
        source_table = jnp.concatenate([own_rows, remote.reshape(-1, coefficients)], 0)
        source_ids = lax.dynamic_slice_in_dim(sources, device * op_count, op_count, 0)
        picked = jnp.where((source_ids >= 0)[:, :, None], source_table[jnp.clip(source_ids, 0, None)], jnp.zeros((), jnp.bfloat16))
        summed = jnp.einsum("okp,opq->kq", picked.astype(jnp.float32), op_float)
        return summed * level_factor

    results = lax.map(one_block, jnp.arange(N_BOX, dtype=jnp.int32))
    return results.reshape(-1, coefficients).astype(jnp.bfloat16)


def reference(exp_fine, req_fine, src_fine, exp_coarse, req_coarse, src_coarse, operators, l2l_ops, relay_src):
    far_fine = far_level(exp_fine, req_fine, src_fine, operators, BF, 1.0)
    far_coarse = far_level(exp_coarse, req_coarse, src_coarse, operators, BC, 0.5)
    children = jnp.einsum("cp,kpq->ckq", far_coarse.astype(jnp.float32), l2l_ops.astype(jnp.float32)).reshape(far_fine.shape)
    relayed = far_fine[relay_src]
    return (children + relayed.astype(jnp.float32)).astype(jnp.bfloat16)
```

```python
import functools

import jax
import jax.numpy as jnp
from jax import lax
from jax.experimental import pallas as pl
from jax.experimental.pallas import tpu as pltpu
from jax.sharding import PartitionSpec as P

R = 32
LANES = 128
COARSE_FACTOR = 0.5
VMEM_LIMIT = 48 << 20


def gather_rows(idx_ref, base, table, out, rows, unroll):
    def step(i, carry):
        first = pl.multiple_of(i * unroll, unroll)
        start = base + first
        picked = [table[pl.ds(idx_ref[start + k], 1), :] for k in range(unroll)]
        for k in range(unroll):
            out[pl.ds(first + k, 1), :] = picked[k]
        return carry

    lax.fori_loop(0, rows // unroll, step, 0)


def widen(source, target, offset, block):
    def step(i, carry):
        first = pl.multiple_of(i * block, block)
        target[pl.ds(offset + first, block), :] = source[pl.ds(first, block), :].astype(jnp.float32)
        return carry

    lax.fori_loop(0, source.shape[0] // block, step, 0)


def pick_kernel(idx_ref, own_ref, out_ref, table, rows):
    step = pl.program_id(0)
    count = own_ref.shape[0]

    @pl.when(step == 0)
    def _():
        widen(own_ref, table, 0, 128)
        table[pl.ds(count, 8), :] = jnp.zeros((8, LANES), jnp.float32)

    block = out_ref.shape[0]
    gather_rows(idx_ref, step * block, table, rows, block, 64)
    out_ref[...] = rows[...].astype(out_ref.dtype)


def pick(own, wanted):
    total, block = wanted.shape[0], 1024
    return pl.pallas_call(
        pick_kernel,
        grid=(total // block,),
        out_shape=jax.ShapeDtypeStruct((total, LANES), own.dtype),
        in_specs=[
            pl.BlockSpec(memory_space=pltpu.SMEM),
            pl.BlockSpec(own.shape, lambda i: (0, 0)),
        ],
        out_specs=pl.BlockSpec((block, LANES), lambda i: (i, 0)),
        scratch_shapes=[
            pltpu.VMEM((own.shape[0] + 8, LANES), jnp.float32),
            pltpu.VMEM((block, LANES), jnp.float32),
        ],
        compiler_params=pltpu.CompilerParams(vmem_limit_bytes=VMEM_LIMIT),
        name="pick",
    )(wanted, own)


def translate_kernel(
    halo_rows, chunk_rows, chunks, ops, idx_ref, own_ref, got_ref, w0, w1, w2, w3, *refs
):
    outs = refs[: 2 if halo_rows else 1]
    table, rows, weights, sems = refs[len(outs) :]
    copies = [
        pltpu.make_async_copy(w, weights.at[g], sems.at[g]) for g, w in enumerate((w0, w1, w2, w3))
    ]
    for copy in copies:
        copy.start()
    own, got = own_ref.shape[0], got_ref.shape[0]
    widen(own_ref, table, 0, 128)
    widen(got_ref, table, own, 512)
    table[pl.ds(own + got, 8), :] = jnp.zeros((8, LANES), jnp.float32)
    for copy in copies:
        copy.wait()

    def summed(base, count, unroll):
        total = jnp.zeros((count, weights.shape[-1]), jnp.float32)
        for g in range(4):
            for o in range(ops):
                gather_rows(idx_ref, base + (g * ops + o) * count, table, rows.at[o], count, unroll)
            left = jnp.concatenate(
                [rows[o, pl.ds(0, count), :].astype(jnp.bfloat16) for o in range(ops)], axis=1
            )
            right = weights[g].reshape(ops * LANES, weights.shape[-1])
            total = total + jnp.dot(left, right, preferred_element_type=jnp.float32)
        return total

    base = 0
    if halo_rows:
        outs[1][...] = summed(0, halo_rows, 64).astype(outs[1].dtype)
        base = 4 * ops * halo_rows

    def chunk(c, carry):
        start = base + c * (4 * ops * chunk_rows)
        outs[0][c] = summed(start, chunk_rows, 96).astype(outs[0].dtype)
        return carry

    lax.fori_loop(0, chunks, chunk, 0)


def translate(idx, own, got, weights, halo_rows, chunk_rows, chunks, dtype):
    ops, _, columns = weights[0].shape
    out_shape = [jax.ShapeDtypeStruct((chunks, chunk_rows, columns), dtype)]
    if halo_rows:
        out_shape.append(jax.ShapeDtypeStruct((halo_rows, columns), dtype))
    vmem = pl.BlockSpec(memory_space=pltpu.VMEM)
    return pl.pallas_call(
        functools.partial(translate_kernel, halo_rows, chunk_rows, chunks, ops),
        out_shape=out_shape,
        in_specs=[pl.BlockSpec(memory_space=pltpu.SMEM), vmem, vmem]
        + [pl.BlockSpec(memory_space=pl.ANY)] * 4,
        out_specs=[vmem] * len(out_shape),
        scratch_shapes=[
            pltpu.VMEM((own.shape[0] + got.shape[0] + 8, LANES), jnp.float32),
            pltpu.VMEM((ops, chunk_rows, LANES), jnp.float32),
            pltpu.VMEM((4, ops, LANES, columns), weights[0].dtype),
            pltpu.SemaphoreType.DMA((4,)),
        ],
        compiler_params=pltpu.CompilerParams(vmem_limit_bytes=VMEM_LIMIT),
        name="translate",
    )(idx, own, got, *weights)


def finish_kernel(own_ref, a_ref, b_ref, c_ref, place_ref, halo_ref, l2l_ref, out_ref, acc):
    quarter = out_ref.shape[0]
    total = own_ref[...] + a_ref[...].astype(jnp.float32)
    total = total + b_ref[...].astype(jnp.float32) + c_ref[...].astype(jnp.float32)
    fine = total[:quarter].astype(jnp.bfloat16).astype(jnp.float32)
    parent = (total[quarter:] * COARSE_FACTOR).astype(jnp.bfloat16)
    acc[...] = jnp.zeros_like(acc)
    for k in range(8):
        child = jnp.dot(parent, l2l_ref[k], preferred_element_type=jnp.float32)
        for j in range(4):
            acc[j, pl.ds(k, parent.shape[0], stride=8), :] = child[:, j * LANES : (j + 1) * LANES]
    halo = halo_ref.shape[0]
    spread = (lax.broadcasted_iota(jnp.int32, (quarter, halo), 1) == place_ref[...]).astype(
        jnp.bfloat16
    )
    foreign = jnp.dot(spread, halo_ref[...], preferred_element_type=jnp.float32)
    children = jnp.concatenate([acc[j] for j in range(4)], axis=1)
    out_ref[...] = (children + (fine + foreign)).astype(out_ref.dtype)


def finish(own, parts, place, halo, l2l_ops, quarter):
    columns = own.shape[1]
    vmem = pl.BlockSpec(memory_space=pltpu.VMEM)
    return pl.pallas_call(
        finish_kernel,
        out_shape=jax.ShapeDtypeStruct((quarter, columns), jnp.bfloat16),
        in_specs=[vmem] * 7,
        out_specs=vmem,
        scratch_shapes=[pltpu.VMEM((columns // LANES, quarter, LANES), jnp.float32)],
        compiler_params=pltpu.CompilerParams(vmem_limit_bytes=VMEM_LIMIT),
        name="finish",
    )(own, *parts, place, halo, l2l_ops)


def per_device(
    exp_fine, req_fine, src_fine, exp_coarse, req_coarse, src_coarse, operators, l2l_ops, relay_src
):
    members = lax.axis_size("grp")
    me = lax.axis_index("grp")
    blocks = lax.axis_size("box")
    here = lax.axis_index("box")
    rows_f, rows_c = exp_fine.shape[0], exp_coarse.shape[0]
    slots_f, slots_c = req_fine.shape[1], req_coarse.shape[1]
    slots = slots_f + slots_c
    own_rows = rows_f + rows_c
    zero_row = own_rows + blocks * slots
    ops, coefficients, _ = operators.shape

    def shifted(value, by):
        return lax.ppermute(value, "grp", [(i, (i + by) % members) for i in range(members)])

    requests = jnp.concatenate(
        [
            jnp.where(req_fine >= 0, req_fine, own_rows),
            jnp.where(req_coarse >= 0, req_coarse + rows_f, own_rows),
        ],
        axis=1,
    )
    wanted = lax.all_to_all(requests[:, None, :], "box", split_axis=0, concat_axis=0, tiled=True)
    first = me * LANES
    own = jnp.concatenate(
        [
            lax.dynamic_slice_in_dim(exp_fine, first, LANES, 1),
            lax.dynamic_slice_in_dim(exp_coarse, first, LANES, 1),
        ],
        axis=0,
    )
    sent = pick(own, wanted.reshape(-1)).reshape(blocks, slots, LANES)
    got = lax.all_to_all(sent, "box", split_axis=0, concat_axis=0, tiled=True)
    got = got.reshape(blocks * slots, LANES)

    by_member = operators.reshape(ops, members, LANES, coefficients)

    def rows_for(member):
        return lax.dynamic_index_in_dim(by_member, member % members, 1, keepdims=False)

    weights = [rows_for(me)] + [shifted(rows_for(me + s), s) for s in range(1, members)]

    q = src_fine - rows_f
    table_f = jnp.where(
        src_fine < rows_f, src_fine, own_rows + (q // slots_f) * slots + q % slots_f
    )
    table_f = jnp.where(src_fine >= 0, table_f, zero_row)
    q = src_coarse - rows_c
    table_c = jnp.where(
        src_coarse < rows_c,
        src_coarse + rows_f,
        own_rows + (q // slots_c) * slots + slots_f + q % slots_c,
    )
    table_c = jnp.where(src_coarse >= 0, table_c, zero_row)
    local = relay_src - here * rows_f
    inside = (local >= 0) & (local < rows_f)
    relayed = jnp.take(table_f.T, jnp.clip(local, 0, rows_f - 1), axis=0).T
    relayed = jnp.where(inside[None, :], relayed, zero_row)
    quarter = rows_f // members
    chunked = jnp.concatenate(
        [relayed.reshape(ops, members, quarter), table_c.reshape(ops, members, rows_c // members)],
        axis=2,
    )
    chunk_rows = chunked.shape[2]
    halo_idx = jnp.concatenate([table_f[:, :R], table_f[:, rows_f - R :]], axis=1)
    packed = jnp.concatenate([chunked.reshape(ops, -1), halo_idx], axis=1)
    every = jnp.stack([packed] + [shifted(packed, s) for s in range(1, members)])
    every_chunk = every[:, :, : members * chunk_rows].reshape(members * ops, members, chunk_rows)

    def chunk_of(member):
        return lax.dynamic_index_in_dim(every_chunk, member % members, 1, keepdims=False).reshape(-1)

    idx_away = jnp.concatenate(
        [every[:, :, members * chunk_rows :].reshape(-1)] + [chunk_of(me + s) for s in range(1, members)]
    )
    idx_here = chunk_of(me)

    away, halo = translate(
        idx_away, own, got, weights, 2 * R, chunk_rows, members - 1, jnp.bfloat16
    )
    parts = [shifted(away[s - 1], s) for s in range(1, members)]
    halo_sum = halo.astype(jnp.float32)
    for s in range(1, members):
        halo_sum = halo_sum + shifted(halo, s).astype(jnp.float32)
    edge = halo_sum.astype(jnp.bfloat16)
    from_left = lax.ppermute(edge[R:], "box", [(i, i + 1) for i in range(blocks - 1)])
    from_right = lax.ppermute(edge[:R], "box", [(i + 1, i) for i in range(blocks - 1)])
    (mine,) = translate(idx_here, own, got, weights, 0, chunk_rows, 1, jnp.float32)

    place = jnp.where(local < 0, local + R, jnp.where(local >= rows_f, local - rows_f + R, -1))
    place = lax.dynamic_slice_in_dim(place, me * quarter, quarter, 0)[:, None]
    done = finish(
        mine[0], parts, place, jnp.concatenate([from_left, from_right], axis=0), l2l_ops, quarter
    )
    out = jnp.zeros((rows_f, coefficients), jnp.bfloat16)
    for s in range(members):
        piece = done if s == 0 else shifted(done, s)
        out = lax.dynamic_update_slice_in_dim(out, piece, ((me - s) % members) * quarter, 0)
    return out


def solution(mesh):
    return jax.shard_map(
        per_device,
        mesh=mesh,
        in_specs=(
            P("box", None),
            P("box", None),
            P(("box", "grp"), None),
            P("box", None),
            P("box", None),
            P(("box", "grp"), None),
            P("grp", None, None),
            P(),
            P("box"),
        ),
        out_specs=P("box", None),
        check_vma=False,
    )
```

```python
import functools

import jax
import jax.numpy as jnp
from jax import lax
from jax.experimental import pallas as pl
from jax.experimental.pallas import tpu as pltpu
from jax.sharding import PartitionSpec as P

R = 32
LANES = 128
COARSE_FACTOR = 0.5
VMEM_LIMIT = 48 << 20


def widen(source, target, block):
    def step(i, carry):
        first = pl.multiple_of(i * block, block)
        target[pl.ds(first, block), :] = source[pl.ds(first, block), :].astype(jnp.float32)
        return carry

    lax.fori_loop(0, source.shape[0] // block, step, 0)


def gather_rows(lists, table, out, count, unroll):
    def step(i, carry):
        for k in range(unroll):
            r = i * unroll + k
            picked = [table[pl.ds(entries[0, r], 1), :] for entries in lists]
            for s, row in enumerate(picked):
                out[s, pl.ds(r, 1), :] = row
        return carry

    lax.fori_loop(0, count // unroll, step, 0)


def pick_kernel(wanted_ref, own_ref, out_ref, table, rows, sem, *lists):
    copies = [pltpu.make_async_copy(wanted_ref.at[s], entries, sem) for s, entries in enumerate(lists)]
    for copy in copies:
        copy.start()
    count = own_ref.shape[0]
    widen(own_ref, table, 128)
    table[pl.ds(count, 8), :] = jnp.zeros((8, LANES), jnp.float32)
    for copy in copies:
        copy.wait()
    gather_rows(lists, table, rows, rows.shape[1], 2)

    def narrow(s, carry):
        out_ref[s] = rows[s].astype(out_ref.dtype)
        return carry

    lax.fori_loop(0, len(lists), narrow, 0)


def pick(own, wanted):
    parts, _, length = wanted.shape
    vmem = pl.BlockSpec(memory_space=pltpu.VMEM)
    return pl.pallas_call(
        pick_kernel,
        out_shape=jax.ShapeDtypeStruct((parts, length, LANES), own.dtype),
        in_specs=[pl.BlockSpec(memory_space=pl.ANY), vmem],
        out_specs=vmem,
        scratch_shapes=[
            pltpu.VMEM((own.shape[0] + 8, LANES), jnp.float32),
            pltpu.VMEM((parts, length, LANES), jnp.float32),
            pltpu.SemaphoreType.DMA,
        ]
        + [pltpu.SMEM((1, length), jnp.int32)] * parts,
        compiler_params=pltpu.CompilerParams(vmem_limit_bytes=VMEM_LIMIT),
        cost_estimate=pl.CostEstimate(
            flops=0, bytes_accessed=2 * parts * length * LANES * 8, transcendentals=0
        ),
        name="pick",
    )(wanted, own)


def operator_sum(rows, weights, count):
    operators, _, columns = weights.shape
    total = jnp.zeros((count, columns), jnp.float32)
    together = 8
    for first in range(0, operators, together):
        left = jnp.concatenate(
            [rows[first + o, pl.ds(0, count), :].astype(jnp.bfloat16) for o in range(together)],
            axis=1,
        )
        right = weights[pl.ds(first, together)].reshape(together * LANES, columns)
        total = total + jnp.dot(left, right, preferred_element_type=jnp.float32)
    return total


def translate_kernel(shifts, halo, pieces, idx_ref, me_ref, own_ref, got_ref, w0, w1, w2, w3, *refs):
    out_ref, table, landed, rows, weights, got_sem, list_sem, weight_sem = refs[:8]
    lists = refs[8:]
    operators, chunk = rows.shape[:2]
    members = 4
    ops = operators // members
    own, got = own_ref.shape[0], got_ref.shape[0]
    piece = got // pieces
    me = me_ref[0]
    arrivals = [
        pltpu.make_async_copy(
            got_ref.at[pl.ds(n * piece, piece), :], landed.at[pl.ds(n * piece, piece), :], got_sem.at[n]
        )
        for n in range(pieces)
    ]
    stride = (idx_ref.shape[2] - LANES) // members
    sets = [(pl.multiple_of(lax.rem(me + s, members) * stride, LANES), chunk) for s in shifts]
    if halo:
        sets = [(members * stride, halo)] + sets
    copies = []
    for n, (first, _) in enumerate(sets):
        batch = []
        for o in range(operators):
            entries = lists[n * operators + o]
            source = idx_ref.at[o, :, pl.ds(first, entries.shape[1])]
            batch.append(pltpu.make_async_copy(source, entries, list_sem.at[n]))
        copies.append(batch)
    heavy = []
    for s, ref in enumerate((w0, w1, w2, w3)):
        heavy.append(pltpu.make_async_copy(ref, weights.at[pl.ds(s * ops, ops)], weight_sem))
    for copy in arrivals + copies[0] + heavy:
        copy.start()
    for batch in copies[1:]:
        for copy in batch:
            copy.start()
    widen(own_ref, table, 128)
    table[pl.ds(own + got, 8), :] = jnp.zeros((8, LANES), jnp.float32)
    for n, copy in enumerate(arrivals):
        copy.wait()
        widen(
            landed.at[pl.ds(n * piece, piece), :], table.at[pl.ds(own + n * piece, piece), :], 512
        )
    for n, (_, count) in enumerate(sets):
        for copy in copies[n]:
            copy.wait()
        gather_rows(lists[n * operators : (n + 1) * operators], table, rows, count, 4)
        if n == 0:
            for copy in heavy:
                copy.wait()
        total = operator_sum(rows, weights, count).astype(out_ref.dtype)
        if halo and n == 0:
            for m in range(len(shifts)):
                out_ref[m, pl.ds(chunk, halo), :] = total
        else:
            out_ref[n - (1 if halo else 0), pl.ds(0, chunk), :] = total


def translate(idx, me, own, got, weights, chunk, shifts, halo, dtype):
    operators, columns = idx.shape[0], weights[0].shape[2]
    vmem = pl.BlockSpec(memory_space=pltpu.VMEM)
    hbm = pl.BlockSpec(memory_space=pltpu.HBM)
    pieces = 4
    stride = (idx.shape[2] - LANES) // 4
    lengths = ([LANES] if halo else []) + [stride] * len(shifts)
    return pl.pallas_call(
        functools.partial(translate_kernel, shifts, halo, pieces),
        out_shape=jax.ShapeDtypeStruct((len(shifts), chunk + halo, columns), dtype),
        in_specs=[hbm, pl.BlockSpec(memory_space=pltpu.SMEM), vmem, hbm] + [hbm] * 4,
        out_specs=vmem,
        scratch_shapes=[
            pltpu.VMEM((own.shape[0] + got.shape[0] + 8, LANES), jnp.float32),
            pltpu.VMEM(got.shape, got.dtype),
            pltpu.VMEM((operators, chunk, LANES), jnp.float32),
            pltpu.VMEM((operators, LANES, columns), weights[0].dtype),
            pltpu.SemaphoreType.DMA((pieces,)),
            pltpu.SemaphoreType.DMA((len(lengths),)),
            pltpu.SemaphoreType.DMA,
        ]
        + [pltpu.SMEM((1, length), jnp.int32) for length in lengths for _ in range(operators)],
        compiler_params=pltpu.CompilerParams(vmem_limit_bytes=VMEM_LIMIT),
        cost_estimate=pl.CostEstimate(
            flops=2 * operators * LANES * columns * chunk * len(shifts),
            bytes_accessed=2 * operators * (chunk * len(shifts) + halo) * LANES * 8,
            transcendentals=0,
        ),
        name="translate",
    )(idx, me, own, got, *weights)


def children_kernel(own_ref, a_ref, b_ref, c_ref, l2l_ref, out_ref, acc):
    count = out_ref.shape[0] // l2l_ref.shape[0]
    first = own_ref.shape[1] - count
    total = own_ref[0, pl.ds(first, count), :]
    for ref in (a_ref, b_ref, c_ref):
        total = total + ref[pl.ds(first, count), :].astype(jnp.float32)
    parent = (total * COARSE_FACTOR).astype(jnp.bfloat16)
    slabs = acc.shape[0]
    for k in range(l2l_ref.shape[0]):
        child = jnp.dot(parent, l2l_ref[k], preferred_element_type=jnp.float32)
        for j in range(slabs):
            acc[j, pl.ds(k, parent.shape[0], stride=l2l_ref.shape[0]), :] = child[
                :, j * LANES : (j + 1) * LANES
            ]
    for j in range(slabs):
        out_ref[:, j * LANES : (j + 1) * LANES] = acc[j]


def children_of(own, parts, l2l_ops, rows):
    columns = l2l_ops.shape[1]
    vmem = pl.BlockSpec(memory_space=pltpu.VMEM)
    return pl.pallas_call(
        children_kernel,
        out_shape=jax.ShapeDtypeStruct((rows, columns), jnp.float32),
        in_specs=[vmem] * 5,
        out_specs=vmem,
        scratch_shapes=[pltpu.VMEM((columns // LANES, rows, LANES), jnp.float32)],
        compiler_params=pltpu.CompilerParams(vmem_limit_bytes=VMEM_LIMIT),
        name="children",
    )(own, *parts, l2l_ops)


def finish_kernel(own_ref, a_ref, b_ref, c_ref, place_ref, left_ref, right_ref, child_ref, out_ref):
    rows = out_ref.shape[0]
    total = own_ref[0, pl.ds(0, rows), :]
    for ref in (a_ref, b_ref, c_ref):
        total = total + ref[pl.ds(0, rows), :].astype(jnp.float32)
    fine = total.astype(jnp.bfloat16).astype(jnp.float32)
    halo = jnp.concatenate([left_ref[...], right_ref[...]], axis=0)
    spread = (
        lax.broadcasted_iota(jnp.int32, (rows, halo.shape[0]), 1) == place_ref[...]
    ).astype(jnp.bfloat16)
    foreign = jnp.dot(spread, halo, preferred_element_type=jnp.float32)
    out_ref[...] = (child_ref[...] + (fine + foreign)).astype(out_ref.dtype)


def finish(own, parts, place, left, right, children):
    vmem = pl.BlockSpec(memory_space=pltpu.VMEM)
    return pl.pallas_call(
        finish_kernel,
        out_shape=jax.ShapeDtypeStruct(children.shape, jnp.bfloat16),
        in_specs=[vmem] * 8,
        out_specs=vmem,
        compiler_params=pltpu.CompilerParams(vmem_limit_bytes=VMEM_LIMIT),
        name="finish",
    )(own, *parts, place, left, right, children)


def per_device(
    exp_fine, req_fine, src_fine, exp_coarse, req_coarse, src_coarse, operators, l2l_ops, relay_src
):
    members = lax.axis_size("grp")
    me = lax.axis_index("grp")
    blocks = lax.axis_size("box")
    here = lax.axis_index("box")
    rows_f, rows_c = exp_fine.shape[0], exp_coarse.shape[0]
    slots_f, slots_c = req_fine.shape[1], req_coarse.shape[1]
    own_rows, slots = rows_f + rows_c, slots_f + slots_c
    zero_row = own_rows + blocks * slots
    ops, coefficients, _ = operators.shape
    quarter_f, quarter_c = rows_f // members, rows_c // members
    chunk = quarter_f + quarter_c
    me_arg = me[None].astype(jnp.int32)

    def shifted(value, by):
        return lax.ppermute(value, "grp", [(i, (i + by) % members) for i in range(members)])

    requests = jnp.concatenate(
        [
            jnp.where(req_fine >= 0, req_fine, own_rows),
            jnp.where(req_coarse >= 0, req_coarse + rows_f, own_rows),
        ],
        axis=1,
    )[:, None, :]
    wanted = lax.all_to_all(requests, "box", split_axis=0, concat_axis=0, tiled=True)
    own = jnp.concatenate(
        [
            lax.dynamic_slice_in_dim(exp_fine, me * LANES, LANES, 1),
            lax.dynamic_slice_in_dim(exp_coarse, me * LANES, LANES, 1),
        ],
        axis=0,
    )
    raw = jnp.concatenate([src_fine, src_coarse], axis=1)
    own, raw = lax.optimization_barrier((own, raw))
    raws = [raw] + [shifted(raw, s) for s in range(1, members)]
    sent = pick(own, wanted)
    sent, raws = lax.optimization_barrier((sent, raws))
    got = lax.all_to_all(sent, "box", split_axis=0, concat_axis=0, tiled=True)
    got = got.reshape(blocks * slots, LANES)

    by_member = operators.reshape(ops, members, LANES, coefficients)

    def rows_for(member):
        return lax.dynamic_index_in_dim(by_member, member % members, 1, keepdims=False)

    weights = [rows_for(me)] + [shifted(rows_for(me + s), s) for s in range(1, members)]

    raw = jnp.concatenate(raws, axis=0)
    src_f, src_c = raw[:, :rows_f], raw[:, rows_f:]
    q = src_f - rows_f
    table_f = jnp.where(src_f < rows_f, src_f, own_rows + (q // slots_f) * slots + q % slots_f)
    table_f = jnp.where(src_f >= 0, table_f, zero_row)
    q = src_c - rows_c
    table_c = own_rows + (q // slots_c) * slots + slots_f + q % slots_c
    table_c = jnp.where(src_c < rows_c, src_c + rows_f, table_c)
    table_c = jnp.where(src_c >= 0, table_c, zero_row)
    local = relay_src - here * rows_f
    inside = (local >= 0) & (local < rows_f)
    relayed = jnp.take(table_f.T, jnp.clip(local, 0, rows_f - 1), axis=0).T
    relayed = jnp.where(inside[None, :], relayed, zero_row)
    every = members * ops
    gap = -chunk % LANES
    chunks = jnp.concatenate(
        [
            relayed.reshape(every, members, quarter_f),
            table_c.reshape(every, members, quarter_c),
            jnp.full((every, members, gap), zero_row, jnp.int32),
        ],
        axis=2,
    )
    idx = jnp.concatenate(
        [
            chunks.reshape(every, -1),
            table_f[:, :R],
            table_f[:, rows_f - R :],
            jnp.full((every, LANES - 2 * R), zero_row, jnp.int32),
        ],
        axis=1,
    )[:, None, :]
    place = jnp.where(local < 0, local + R, jnp.where(local >= rows_f, local - rows_f + R, -1))
    place = lax.dynamic_slice_in_dim(place, me * quarter_f, quarter_f, 0)[:, None]
    got, place, idx = lax.optimization_barrier((got, place, idx))

    def sums(shifts, halo, dtype):
        return translate(idx, me_arg, own, got, weights, chunk, shifts, halo, dtype)

    away = sums((2, 1, 3), 2 * R, jnp.bfloat16)
    others = [shifted(away[n], s) for n, s in enumerate((2, 1, 3))]
    mine = sums((0,), 0, jnp.float32)
    others, mine = lax.optimization_barrier((others, mine))
    edge = away[0, chunk:].astype(jnp.float32)
    for other in others:
        edge = edge + other[chunk:].astype(jnp.float32)
    edge = edge.astype(jnp.bfloat16)
    from_left = lax.ppermute(edge[R:], "box", [(i, i + 1) for i in range(blocks - 1)])
    from_right = lax.ppermute(edge[:R], "box", [(i + 1, i) for i in range(blocks - 1)])
    children = children_of(mine, others, l2l_ops, quarter_f)
    done = finish(mine, others, place, from_left, from_right, children)
    out = jnp.zeros((rows_f, coefficients), jnp.bfloat16)
    for s in range(members):
        piece = done if s == 0 else shifted(done, s)
        out = lax.dynamic_update_slice_in_dim(out, piece, ((me - s) % members) * quarter_f, 0)
    return out


def solution(mesh):
    return jax.shard_map(
        per_device,
        mesh=mesh,
        in_specs=(
            P("box", None),
            P("box", None),
            P(("box", "grp"), None),
            P("box", None),
            P("box", None),
            P(("box", "grp"), None),
            P("grp", None, None),
            P(),
            P("box"),
        ),
        out_specs=P("box", None),
        check_vma=False,
    )
```

```python
import functools

import jax
import jax.numpy as jnp
from jax import lax
from jax.experimental import pallas as pl
from jax.experimental.pallas import tpu as pltpu
from jax.sharding import PartitionSpec as P

R = 32
LANES = 128
CORES = 2
COARSE_FACTOR = 0.5
VMEM_LIMIT = 48 << 20


def widen(source, target, block):
    def step(i, carry):
        first = pl.multiple_of(i * block, block)
        target[pl.ds(first, block), :] = source[pl.ds(first, block), :].astype(jnp.float32)
        return carry

    lax.fori_loop(0, source.shape[0] // block, step, 0)


def gather_rows(lists, table, out, count, unroll):
    def step(i, carry):
        for k in range(unroll):
            r = i * unroll + k
            picked = [table[pl.ds(entries[0, r], 1), :] for entries in lists]
            for s, row in enumerate(picked):
                out[s, pl.ds(r, 1), :] = row
        return carry

    lax.fori_loop(0, count // unroll, step, 0)


def pick_kernel(wanted_ref, own_ref, out_ref, table, rows, sem, *lists):
    copies = [pltpu.make_async_copy(wanted_ref.at[s], entries, sem) for s, entries in enumerate(lists)]
    for copy in copies:
        copy.start()
    count = own_ref.shape[0]
    widen(own_ref, table, 128)
    table[pl.ds(count, 8), :] = jnp.zeros((8, LANES), jnp.float32)
    for copy in copies:
        copy.wait()
    gather_rows(lists, table, rows, rows.shape[1], 2)

    def narrow(s, carry):
        out_ref[s] = rows[s].astype(out_ref.dtype)
        return carry

    lax.fori_loop(0, len(lists), narrow, 0)


def pick(own, wanted):
    parts, _, length = wanted.shape
    vmem = pl.BlockSpec(memory_space=pltpu.VMEM)
    return pl.pallas_call(
        pick_kernel,
        out_shape=jax.ShapeDtypeStruct((parts, length, LANES), own.dtype),
        in_specs=[pl.BlockSpec(memory_space=pl.ANY), vmem],
        out_specs=vmem,
        scratch_shapes=[
            pltpu.VMEM((own.shape[0] + 8, LANES), jnp.float32),
            pltpu.VMEM((parts, length, LANES), jnp.float32),
            pltpu.SemaphoreType.DMA,
        ]
        + [pltpu.SMEM((1, length), jnp.int32)] * parts,
        compiler_params=pltpu.CompilerParams(vmem_limit_bytes=VMEM_LIMIT),
        cost_estimate=pl.CostEstimate(
            flops=0, bytes_accessed=2 * parts * length * LANES * 8, transcendentals=0
        ),
        name="pick",
    )(wanted, own)


def operator_sum(rows, weights, count):
    operators, _, columns = weights.shape
    total = jnp.zeros((count, columns), jnp.float32)
    together = 8
    for first in range(0, operators, together):
        left = jnp.concatenate(
            [rows[first + o, pl.ds(0, count), :].astype(jnp.bfloat16) for o in range(together)],
            axis=1,
        )
        right = weights[pl.ds(first, together)].reshape(together * LANES, columns)
        total = total + jnp.dot(left, right, preferred_element_type=jnp.float32)
    return total


def translate_kernel(shifts, halo, idx_ref, at_ref, own_ref, got_ref, ops_ref, *refs):
    weight_refs, refs = refs[:6], refs[6:]
    outs, refs = refs[: len(shifts)], refs[len(shifts) :]
    table, landed, rows, weights, got_sem, list_sem, weight_sem = refs[:7]
    lists = refs[7:]
    operators, chunk = rows.shape[:2]
    members, ops = 4, ops_ref.shape[0]
    me, core = at_ref[0], at_ref[1]
    own, got = own_ref.shape[0], landed.shape[0]
    piece = got // got_sem.shape[0]
    arrivals = []
    for n in range(got // piece):
        part = pl.ds(n * piece, piece)
        arrivals.append(
            pltpu.make_async_copy(got_ref.at[part, :], landed.at[part, :], got_sem.at[n])
        )
    stride = (idx_ref.shape[2] - LANES) // members
    sets = [(pl.multiple_of(lax.rem(me + s, members) * stride, LANES), chunk) for s in shifts]
    if halo:
        sets = [(members * stride, halo)] + sets
    copies = []
    for n, (start, _) in enumerate(sets):
        batch = []
        for o in range(operators):
            entries = lists[n * operators + o]
            source = idx_ref.at[o, :, pl.ds(start, entries.shape[1])]
            batch.append(pltpu.make_async_copy(source, entries, list_sem.at[n]))
        copies.append(batch)
    columns = pl.ds(pl.multiple_of(me * LANES, LANES), LANES)
    heavy = [
        pltpu.make_async_copy(ops_ref.at[:, columns, :], weights.at[pl.ds(0, ops)], weight_sem)
    ]
    half = ops // 2
    for n, ref in enumerate(weight_refs):
        side = core if n % 2 == 0 else 1 - core
        place = weights.at[pl.ds((n // 2 + 1) * ops + side * half, half)]
        heavy.append(pltpu.make_async_copy(ref, place, weight_sem))
    for copy in arrivals + copies[0] + heavy:
        copy.start()
    for batch in copies[1:]:
        for copy in batch:
            copy.start()
    widen(own_ref, table, 128)
    table[pl.ds(own + got, 8), :] = jnp.zeros((8, LANES), jnp.float32)
    for n, copy in enumerate(arrivals):
        copy.wait()
        widen(
            landed.at[pl.ds(n * piece, piece), :], table.at[pl.ds(own + n * piece, piece), :], 512
        )
    for n, (_, count) in enumerate(sets):
        for copy in copies[n]:
            copy.wait()
        chosen = lists[n * operators : (n + 1) * operators]
        edge_rows = halo and n == 0
        gather_rows(chosen, table, rows, count, 4)
        if n == 0:
            for copy in heavy:
                copy.wait()
        total = operator_sum(rows, weights, count).astype(outs[0].dtype)
        if edge_rows:
            for out in outs:
                out[pl.ds(chunk, halo), :] = total
        else:
            outs[n - (1 if halo else 0)][pl.ds(0, chunk), :] = total


def translate(idx, at, own, got, operators, weights, chunk, shifts, halo, dtype):
    every, columns = idx.shape[0], operators.shape[2]
    vmem = pl.BlockSpec(memory_space=pltpu.VMEM)
    hbm = pl.BlockSpec(memory_space=pltpu.HBM)
    stride = (idx.shape[2] - LANES) // 4
    lengths = ([LANES] if halo else []) + [stride] * len(shifts)
    return pl.pallas_call(
        functools.partial(translate_kernel, shifts, halo),
        out_shape=[jax.ShapeDtypeStruct((chunk + halo, columns), dtype)] * len(shifts),
        in_specs=[hbm, pl.BlockSpec(memory_space=pltpu.SMEM), vmem] + [hbm] * (2 + len(weights)),
        out_specs=[vmem] * len(shifts),
        scratch_shapes=[
            pltpu.VMEM((own.shape[0] + got.shape[0] + 8, LANES), jnp.float32),
            pltpu.VMEM(got.shape, own.dtype),
            pltpu.VMEM((every, chunk, LANES), jnp.float32),
            pltpu.VMEM((every, LANES, columns), operators.dtype),
            pltpu.SemaphoreType.DMA((4,)),
            pltpu.SemaphoreType.DMA((len(lengths),)),
            pltpu.SemaphoreType.DMA,
        ]
        + [pltpu.SMEM((1, length), jnp.int32) for length in lengths for _ in range(every)],
        compiler_params=pltpu.CompilerParams(vmem_limit_bytes=VMEM_LIMIT),
        cost_estimate=pl.CostEstimate(
            flops=2 * every * LANES * columns * chunk * len(shifts),
            bytes_accessed=2 * every * (chunk * len(shifts) + halo) * LANES * 8,
            transcendentals=0,
        ),
        name="translate",
    )(idx, at, own, got, operators, *weights)


def edge_kernel(own_ref, a_ref, b_ref, c_ref, head_ref, tail_ref):
    half = head_ref.shape[0]
    for out, last in ((head_ref, 2 * half), (tail_ref, half)):
        total = jnp.zeros(out.shape, jnp.float32)
        for ref in (own_ref, a_ref, b_ref, c_ref):
            total = total + ref[pl.ds(ref.shape[0] - last, half), :].astype(jnp.float32)
        out[...] = total.astype(out.dtype)


def edges(parts, halo):
    half = jax.ShapeDtypeStruct((halo // 2, parts[0].shape[1]), parts[0].dtype)
    vmem = pl.BlockSpec(memory_space=pltpu.VMEM)
    return pl.pallas_call(
        edge_kernel,
        out_shape=[half, half],
        in_specs=[vmem] * 4,
        out_specs=[vmem] * 2,
        compiler_params=pltpu.CompilerParams(vmem_limit_bytes=VMEM_LIMIT),
        name="edges",
    )(*parts)


def finish_kernel(
    own_ref, a_ref, b_ref, c_ref, place_ref, left_ref, right_ref, l2l_ref, out_ref, acc
):
    rows, columns = out_ref.shape
    octants = l2l_ref.shape[0]
    count = rows // octants

    def total(first, size):
        part = own_ref[pl.ds(first, size), :]
        for ref in (a_ref, b_ref, c_ref):
            part = part + ref[pl.ds(first, size), :].astype(jnp.float32)
        return part

    parent = (total(rows, count) * COARSE_FACTOR).astype(jnp.bfloat16)
    slabs = columns // LANES
    for k in range(octants):
        child = jnp.dot(parent, l2l_ref[k], preferred_element_type=jnp.float32)
        for j in range(slabs):
            acc[j, pl.ds(k, count, stride=octants), :] = child[:, j * LANES : (j + 1) * LANES]
    fine = total(0, rows).astype(jnp.bfloat16).astype(jnp.float32)
    halo = jnp.concatenate([left_ref[...], right_ref[...]], axis=0)
    spread = (
        lax.broadcasted_iota(jnp.int32, (halo.shape[0], rows), 0) == place_ref[...]
    ).astype(jnp.bfloat16)
    foreign = lax.dot_general(
        spread, halo, (((0,), (0,)), ((), ())), preferred_element_type=jnp.float32
    )
    far = fine + foreign
    for j in range(slabs):
        lanes = slice(j * LANES, (j + 1) * LANES)
        out_ref[:, lanes] = (acc[j] + far[:, lanes]).astype(out_ref.dtype)


def finish(own, parts, place, left, right, l2l_ops):
    rows, columns = place.shape[1], own.shape[1]
    vmem = pl.BlockSpec(memory_space=pltpu.VMEM)
    return pl.pallas_call(
        finish_kernel,
        out_shape=jax.ShapeDtypeStruct((rows, columns), jnp.bfloat16),
        in_specs=[vmem] * 8,
        out_specs=vmem,
        scratch_shapes=[pltpu.VMEM((columns // LANES, rows, LANES), jnp.float32)],
        compiler_params=pltpu.CompilerParams(vmem_limit_bytes=VMEM_LIMIT),
        name="finish",
    )(own, *parts, place, left, right, l2l_ops)


def per_device(
    exp_fine, req_fine, src_fine, exp_coarse, req_coarse, src_coarse, operators, l2l_ops, relay_src
):
    members = lax.axis_size("grp")
    me = lax.axis_index("grp")
    blocks = lax.axis_size("box")
    here = lax.axis_index("box")
    rows_f, rows_c = exp_fine.shape[0], exp_coarse.shape[0]
    slots_f, slots_c = req_fine.shape[1], req_coarse.shape[1]
    own_rows, slots = rows_f + rows_c, slots_f + slots_c
    zero_row = own_rows + blocks * slots
    ops, coefficients, _ = operators.shape
    quarter_f, quarter_c = rows_f // members, rows_c // members
    chunk = quarter_f + quarter_c
    at = jnp.stack([me, here % CORES]).astype(jnp.int32)

    def shifted(value, by):
        return lax.ppermute(value, "grp", [(i, (i + by) % members) for i in range(members)])

    def swapped(value):
        return lax.ppermute(value, "box", [(i, i ^ 1) for i in range(blocks)])

    requests = jnp.concatenate(
        [
            jnp.where(req_fine >= 0, req_fine, own_rows),
            jnp.where(req_coarse >= 0, req_coarse + rows_f, own_rows),
        ],
        axis=1,
    )[:, None, :]
    wanted = lax.all_to_all(requests, "box", split_axis=0, concat_axis=0, tiled=True)
    own = jnp.concatenate(
        [
            lax.dynamic_slice_in_dim(exp_fine, me * LANES, LANES, 1),
            lax.dynamic_slice_in_dim(exp_coarse, me * LANES, LANES, 1),
        ],
        axis=0,
    )
    sent = pick(own, wanted)
    got = lax.all_to_all(sent, "box", split_axis=0, concat_axis=0, tiled=True)
    got = got.reshape(blocks * slots, LANES)

    raw = jnp.concatenate([src_fine, src_coarse], axis=1)
    raws = [raw] + [shifted(raw, s) for s in range(1, members)]
    raws, held = lax.optimization_barrier((raws, operators))
    raw = jnp.concatenate(raws, axis=0)

    half = ops // CORES
    weights = []
    for s in range(1, members):
        start = ((here % CORES) * half, ((me + s) % members) * LANES, 0)
        fetched = shifted(lax.dynamic_slice(held, start, (half, LANES, coefficients)), s)
        weights += [fetched, swapped(fetched)]

    src_f, src_c = raw[:, :rows_f], raw[:, rows_f:]
    q = src_f - rows_f
    table_f = jnp.where(src_f < rows_f, src_f, own_rows + (q // slots_f) * slots + q % slots_f)
    table_f = jnp.where(src_f >= 0, table_f, zero_row)
    q = src_c - rows_c
    table_c = own_rows + (q // slots_c) * slots + slots_f + q % slots_c
    table_c = jnp.where(src_c < rows_c, src_c + rows_f, table_c)
    table_c = jnp.where(src_c >= 0, table_c, zero_row)
    local = relay_src - here * rows_f
    inside = (local >= 0) & (local < rows_f)
    relayed = jnp.take(table_f.T, jnp.clip(local, 0, rows_f - 1), axis=0).T
    relayed = jnp.where(inside[None, :], relayed, zero_row)
    every = members * ops
    gap = -chunk % LANES
    chunks = jnp.concatenate(
        [
            relayed.reshape(every, members, quarter_f),
            table_c.reshape(every, members, quarter_c),
            jnp.full((every, members, gap), zero_row, jnp.int32),
        ],
        axis=2,
    )
    idx = jnp.concatenate(
        [
            chunks.reshape(every, -1),
            table_f[:, :R],
            table_f[:, rows_f - R :],
            jnp.full((every, LANES - 2 * R), zero_row, jnp.int32),
        ],
        axis=1,
    )[:, None, :]
    place = jnp.where(local < 0, local + R, jnp.where(local >= rows_f, local - rows_f + R, -1))
    place = lax.dynamic_slice_in_dim(place, me * quarter_f, quarter_f, 0)[None, :]
    got, place, idx = lax.optimization_barrier((got, place, idx))

    def sums(shifts, halo, dtype):
        return translate(idx, at, own, got, operators, weights, chunk, shifts, halo, dtype)

    away = sums((2, 1, 3), 2 * R, jnp.bfloat16)
    others = [shifted(part, s) for part, s in zip(away, (2, 1, 3))]
    (mine,) = sums((0,), 0, jnp.float32)
    others, mine = lax.optimization_barrier((others, mine))
    head, tail = edges([away[0]] + others, 2 * R)
    from_left = lax.ppermute(tail, "box", [(i, i + 1) for i in range(blocks - 1)])
    from_right = lax.ppermute(head, "box", [(i + 1, i) for i in range(blocks - 1)])
    done = finish(mine, others, place, from_left, from_right, l2l_ops)
    out = jnp.zeros((rows_f, coefficients), jnp.bfloat16)
    for s in range(members):
        piece = done if s == 0 else shifted(done, s)
        out = lax.dynamic_update_slice_in_dim(out, piece, ((me - s) % members) * quarter_f, 0)
    return out


def solution(mesh):
    return jax.shard_map(
        per_device,
        mesh=mesh,
        in_specs=(
            P("box", None),
            P("box", None),
            P(("box", "grp"), None),
            P("box", None),
            P("box", None),
            P(("box", "grp"), None),
            P("grp", None, None),
            P(),
            P("box"),
        ),
        out_specs=P("box", None),
        check_vma=False,
    )
```

```python
import functools

import jax
import jax.numpy as jnp
from jax import lax
from jax.experimental import pallas as pl
from jax.experimental.pallas import tpu as pltpu
from jax.sharding import PartitionSpec as P

R = 32
LANES = 128
CORES = 2
COARSE_FACTOR = 0.5
VMEM_LIMIT = 48 << 20


def widen(source, target, block):
    def step(i, carry):
        first = pl.multiple_of(i * block, block)
        target[pl.ds(first, block), :] = source[pl.ds(first, block), :].astype(jnp.float32)
        return carry

    lax.fori_loop(0, source.shape[0] // block, step, 0)


def gather_rows(lists, table, out, count, unroll):
    def step(i, carry):
        for k in range(unroll):
            r = i * unroll + k
            picked = [table[pl.ds(entries[0, r], 1), :] for entries in lists]
            for s, row in enumerate(picked):
                out[s, pl.ds(r, 1), :] = row
        return carry

    lax.fori_loop(0, count // unroll, step, 0)


def pick_kernel(wanted_ref, own_ref, out_ref, table, rows, sem, *lists):
    copies = [pltpu.make_async_copy(wanted_ref.at[s], entries, sem) for s, entries in enumerate(lists)]
    for copy in copies:
        copy.start()
    count = own_ref.shape[0]
    widen(own_ref, table, 128)
    table[pl.ds(count, 8), :] = jnp.zeros((8, LANES), jnp.float32)
    for copy in copies:
        copy.wait()
    gather_rows(lists, table, rows, rows.shape[1], 2)

    def narrow(s, carry):
        out_ref[s] = rows[s].astype(out_ref.dtype)
        return carry

    lax.fori_loop(0, len(lists), narrow, 0)


def pick(own, wanted):
    parts, _, length = wanted.shape
    vmem = pl.BlockSpec(memory_space=pltpu.VMEM)
    return pl.pallas_call(
        pick_kernel,
        out_shape=jax.ShapeDtypeStruct((parts, length, LANES), own.dtype),
        in_specs=[pl.BlockSpec(memory_space=pl.ANY), vmem],
        out_specs=vmem,
        scratch_shapes=[
            pltpu.VMEM((own.shape[0] + 8, LANES), jnp.float32),
            pltpu.VMEM((parts, length, LANES), jnp.float32),
            pltpu.SemaphoreType.DMA,
        ]
        + [pltpu.SMEM((1, length), jnp.int32)] * parts,
        compiler_params=pltpu.CompilerParams(vmem_limit_bytes=VMEM_LIMIT),
        cost_estimate=pl.CostEstimate(
            flops=0, bytes_accessed=2 * parts * length * LANES * 8, transcendentals=0
        ),
        name="pick",
    )(wanted, own)


def operator_sum(rows, weights, count):
    operators, _, columns = weights.shape
    total = jnp.zeros((count, columns), jnp.float32)
    together = 8
    for first in range(0, operators, together):
        left = jnp.concatenate(
            [rows[first + o, pl.ds(0, count), :].astype(jnp.bfloat16) for o in range(together)],
            axis=1,
        )
        right = weights[pl.ds(first, together)].reshape(together * LANES, columns)
        total = total + jnp.dot(left, right, preferred_element_type=jnp.float32)
    return total


def translate_kernel(shifts, halo, idx_ref, at_ref, own_ref, got_ref, ops_ref, *refs):
    weight_refs, refs = refs[:6], refs[6:]
    outs, refs = refs[: len(shifts)], refs[len(shifts) :]
    table, landed, rows, weights, got_sem, list_sem, weight_sem = refs[:7]
    lists = refs[7:]
    operators, chunk = rows.shape[:2]
    members, ops = 4, ops_ref.shape[0]
    me, core = at_ref[0], at_ref[1]
    own, got = own_ref.shape[0], landed.shape[0]
    piece = got // got_sem.shape[0]
    arrivals = []
    for n in range(got // piece):
        part = pl.ds(n * piece, piece)
        arrivals.append(
            pltpu.make_async_copy(got_ref.at[part, :], landed.at[part, :], got_sem.at[n])
        )
    stride = (idx_ref.shape[2] - LANES) // members
    sets = [(pl.multiple_of(lax.rem(me + s, members) * stride, LANES), chunk) for s in shifts]
    if halo:
        sets = [(members * stride, halo)] + sets
    copies = []
    for n, (start, _) in enumerate(sets):
        batch = []
        for o in range(operators):
            entries = lists[n * operators + o]
            source = idx_ref.at[o, :, pl.ds(start, entries.shape[1])]
            batch.append(pltpu.make_async_copy(source, entries, list_sem.at[n]))
        copies.append(batch)
    columns = pl.ds(pl.multiple_of(me * LANES, LANES), LANES)
    heavy = [
        pltpu.make_async_copy(ops_ref.at[:, columns, :], weights.at[pl.ds(0, ops)], weight_sem)
    ]
    half = ops // 2
    for n, ref in enumerate(weight_refs):
        side = core if n % 2 == 0 else 1 - core
        place = weights.at[pl.ds((n // 2 + 1) * ops + side * half, half)]
        heavy.append(pltpu.make_async_copy(ref, place, weight_sem))
    for copy in arrivals + copies[0] + heavy:
        copy.start()
    for batch in copies[1:]:
        for copy in batch:
            copy.start()
    widen(own_ref, table, 128)
    table[pl.ds(own + got, 8), :] = jnp.zeros((8, LANES), jnp.float32)
    for n, copy in enumerate(arrivals):
        copy.wait()
        widen(
            landed.at[pl.ds(n * piece, piece), :], table.at[pl.ds(own + n * piece, piece), :], 512
        )
    for n, (_, count) in enumerate(sets):
        for copy in copies[n]:
            copy.wait()
        chosen = lists[n * operators : (n + 1) * operators]
        edge_rows = halo and n == 0
        gather_rows(chosen, table, rows, count, 8)
        if n == 0:
            for copy in heavy:
                copy.wait()
        total = operator_sum(rows, weights, count)
        if edge_rows:
            for out in outs:
                out[pl.ds(chunk, halo), :] = total.astype(out.dtype)
        else:
            out = outs[n - (1 if halo else 0)]
            out[pl.ds(0, chunk), :] = total.astype(out.dtype)


def translate(idx, at, own, got, operators, weights, chunk, shifts, halo, dtypes):
    every, columns = idx.shape[0], operators.shape[2]
    vmem = pl.BlockSpec(memory_space=pltpu.VMEM)
    hbm = pl.BlockSpec(memory_space=pltpu.HBM)
    stride = (idx.shape[2] - LANES) // 4
    lengths = ([LANES] if halo else []) + [stride] * len(shifts)
    return pl.pallas_call(
        functools.partial(translate_kernel, shifts, halo),
        out_shape=[jax.ShapeDtypeStruct((chunk + halo, columns), dtype) for dtype in dtypes],
        in_specs=[hbm, pl.BlockSpec(memory_space=pltpu.SMEM), vmem] + [hbm] * (2 + len(weights)),
        out_specs=[vmem] * len(shifts),
        scratch_shapes=[
            pltpu.VMEM((own.shape[0] + got.shape[0] + 8, LANES), jnp.float32),
            pltpu.VMEM(got.shape, own.dtype),
            pltpu.VMEM((every, chunk, LANES), jnp.float32),
            pltpu.VMEM((every, LANES, columns), operators.dtype),
            pltpu.SemaphoreType.DMA((4,)),
            pltpu.SemaphoreType.DMA((len(lengths),)),
            pltpu.SemaphoreType.DMA,
        ]
        + [pltpu.SMEM((1, length), jnp.int32) for length in lengths for _ in range(every)],
        compiler_params=pltpu.CompilerParams(vmem_limit_bytes=VMEM_LIMIT),
        cost_estimate=pl.CostEstimate(
            flops=2 * every * LANES * columns * chunk * len(shifts),
            bytes_accessed=2 * every * (chunk * len(shifts) + halo) * LANES * 8,
            transcendentals=0,
        ),
        name="translate",
    )(idx, at, own, got, operators, *weights)


def edge_kernel(own_ref, a_ref, b_ref, c_ref, head_ref, tail_ref):
    half = head_ref.shape[0]
    for out, last in ((head_ref, 2 * half), (tail_ref, half)):
        total = jnp.zeros(out.shape, jnp.float32)
        for ref in (own_ref, a_ref, b_ref, c_ref):
            total = total + ref[pl.ds(ref.shape[0] - last, half), :].astype(jnp.float32)
        out[...] = total.astype(out.dtype)


def edges(parts, halo):
    half = jax.ShapeDtypeStruct((halo // 2, parts[0].shape[1]), parts[0].dtype)
    vmem = pl.BlockSpec(memory_space=pltpu.VMEM)
    return pl.pallas_call(
        edge_kernel,
        out_shape=[half, half],
        in_specs=[vmem] * 4,
        out_specs=[vmem] * 2,
        compiler_params=pltpu.CompilerParams(vmem_limit_bytes=VMEM_LIMIT),
        name="edges",
    )(*parts)


def finish_kernel(
    own_ref, a_ref, b_ref, c_ref, place_ref, left_ref, right_ref, l2l_ref, out_ref, acc
):
    rows, columns = out_ref.shape
    octants = l2l_ref.shape[0]
    count = rows // octants

    def total(first, size):
        part = own_ref[pl.ds(first, size), :]
        for ref in (a_ref, b_ref, c_ref):
            part = part + ref[pl.ds(first, size), :].astype(jnp.float32)
        return part

    parent = (total(rows, count) * COARSE_FACTOR).astype(jnp.bfloat16)
    slabs = columns // LANES
    for k in range(octants):
        child = jnp.dot(parent, l2l_ref[k], preferred_element_type=jnp.float32)
        for j in range(slabs):
            acc[j, pl.ds(k, count, stride=octants), :] = child[:, j * LANES : (j + 1) * LANES]
    fine = total(0, rows).astype(jnp.bfloat16).astype(jnp.float32)
    halo = jnp.concatenate([left_ref[...], right_ref[...]], axis=0)
    spread = (
        lax.broadcasted_iota(jnp.int32, (halo.shape[0], rows), 0) == place_ref[...]
    ).astype(jnp.bfloat16)
    foreign = lax.dot_general(
        spread, halo, (((0,), (0,)), ((), ())), preferred_element_type=jnp.float32
    )
    far = fine + foreign
    for j in range(slabs):
        lanes = slice(j * LANES, (j + 1) * LANES)
        out_ref[:, lanes] = (acc[j] + far[:, lanes]).astype(out_ref.dtype)


def finish(own, parts, place, left, right, l2l_ops):
    rows, columns = place.shape[1], own.shape[1]
    vmem = pl.BlockSpec(memory_space=pltpu.VMEM)
    return pl.pallas_call(
        finish_kernel,
        out_shape=jax.ShapeDtypeStruct((rows, columns), jnp.bfloat16),
        in_specs=[vmem] * 8,
        out_specs=vmem,
        scratch_shapes=[pltpu.VMEM((columns // LANES, rows, LANES), jnp.float32)],
        compiler_params=pltpu.CompilerParams(vmem_limit_bytes=VMEM_LIMIT),
        name="finish",
    )(own, *parts, place, left, right, l2l_ops)


def per_device(
    exp_fine, req_fine, src_fine, exp_coarse, req_coarse, src_coarse, operators, l2l_ops, relay_src
):
    members = lax.axis_size("grp")
    me = lax.axis_index("grp")
    blocks = lax.axis_size("box")
    here = lax.axis_index("box")
    rows_f, rows_c = exp_fine.shape[0], exp_coarse.shape[0]
    slots_f, slots_c = req_fine.shape[1], req_coarse.shape[1]
    own_rows, slots = rows_f + rows_c, slots_f + slots_c
    zero_row = own_rows + blocks * slots
    ops, coefficients, _ = operators.shape
    quarter_f, quarter_c = rows_f // members, rows_c // members
    chunk = quarter_f + quarter_c
    at = jnp.stack([me, here % CORES]).astype(jnp.int32)

    def shifted(value, by):
        return lax.ppermute(value, "grp", [(i, (i + by) % members) for i in range(members)])

    def swapped(value):
        return lax.ppermute(value, "box", [(i, i ^ 1) for i in range(blocks)])

    asked = jnp.concatenate([req_fine, req_coarse], axis=1)[:, None, :]
    starts = jnp.where(jnp.arange(slots) < slots_f, 0, rows_f)
    requests = jnp.where(asked >= 0, asked + starts, own_rows)
    wanted = lax.all_to_all(requests, "box", split_axis=0, concat_axis=0, tiled=True)
    own = jnp.concatenate(
        [
            lax.dynamic_slice_in_dim(exp_fine, me * LANES, LANES, 1),
            lax.dynamic_slice_in_dim(exp_coarse, me * LANES, LANES, 1),
        ],
        axis=0,
    )
    sent = pick(own, wanted)
    got = lax.all_to_all(sent, "box", split_axis=0, concat_axis=0, tiled=True)
    got = got.reshape(blocks * slots, LANES)

    raw = jnp.concatenate([src_fine, src_coarse], axis=1)
    raws = [raw] + [shifted(raw, s) for s in range(1, members)]
    raws, held = lax.optimization_barrier((raws, operators))
    raw = jnp.concatenate(raws, axis=0)

    half = ops // CORES
    weights = []
    for s in range(1, members):
        start = ((here % CORES) * half, ((me + s) % members) * LANES, 0)
        fetched = shifted(lax.dynamic_slice(held, start, (half, LANES, coefficients)), s)
        weights += [fetched, swapped(fetched)]

    src_f, src_c = raw[:, :rows_f], raw[:, rows_f:]
    q = src_f - rows_f
    table_f = jnp.where(src_f < rows_f, src_f, own_rows + (q // slots_f) * slots + q % slots_f)
    table_f = jnp.where(src_f >= 0, table_f, zero_row)
    q = src_c - rows_c
    table_c = own_rows + (q // slots_c) * slots + slots_f + q % slots_c
    table_c = jnp.where(src_c < rows_c, src_c + rows_f, table_c)
    table_c = jnp.where(src_c >= 0, table_c, zero_row)
    local = relay_src - here * rows_f
    inside = (local >= 0) & (local < rows_f)
    relayed = jnp.take(table_f.T, jnp.clip(local, 0, rows_f - 1), axis=0).T
    relayed = jnp.where(inside[None, :], relayed, zero_row)
    every = members * ops
    gap = -chunk % LANES
    chunks = jnp.concatenate(
        [
            relayed.reshape(every, members, quarter_f),
            table_c.reshape(every, members, quarter_c),
            jnp.full((every, members, gap), zero_row, jnp.int32),
        ],
        axis=2,
    )
    idx = jnp.concatenate(
        [
            chunks.reshape(every, -1),
            table_f[:, :R],
            table_f[:, rows_f - R :],
            jnp.full((every, LANES - 2 * R), zero_row, jnp.int32),
        ],
        axis=1,
    )[:, None, :]
    place = jnp.where(local < 0, local + R, jnp.where(local >= rows_f, local - rows_f + R, -1))
    place = lax.dynamic_slice_in_dim(place, me * quarter_f, quarter_f, 0)[None, :]
    got, place, idx = lax.optimization_barrier((got, place, idx))

    def sums(shifts, halo, dtypes):
        return translate(idx, at, own, got, operators, weights, chunk, shifts, halo, dtypes)

    away = sums((2, 1), 2 * R, (jnp.bfloat16, jnp.bfloat16))
    halo_3 = shifted(away[0][chunk:], 3)
    others = [shifted(part, s) for part, s in zip(away, (2, 1))]
    last, mine = sums((3, 0), 0, (jnp.bfloat16, jnp.float32))
    others, halo_3, last, mine = lax.optimization_barrier((others, halo_3, last, mine))
    head, tail = edges([away[0]] + others + [halo_3], 2 * R)
    from_left = lax.ppermute(tail, "box", [(i, i + 1) for i in range(blocks - 1)])
    from_right = lax.ppermute(head, "box", [(i + 1, i) for i in range(blocks - 1)])
    others = others + [shifted(last, 3)]
    done = finish(mine, others, place, from_left, from_right, l2l_ops)
    out = jnp.zeros((rows_f, coefficients), jnp.bfloat16)
    for s in (0, 2, 1, 3):
        piece = done if s == 0 else shifted(done, s)
        out = lax.dynamic_update_slice_in_dim(out, piece, ((me - s) % members) * quarter_f, 0)
    return out


def solution(mesh):
    return jax.shard_map(
        per_device,
        mesh=mesh,
        in_specs=(
            P("box", None),
            P("box", None),
            P(("box", "grp"), None),
            P("box", None),
            P("box", None),
            P(("box", "grp"), None),
            P("grp", None, None),
            P(),
            P("box"),
        ),
        out_specs=P("box", None),
        check_vma=False,
    )
```

```python
import functools

import jax
import jax.numpy as jnp
from jax import lax
from jax.experimental import pallas as pl
from jax.experimental.pallas import tpu as pltpu
from jax.sharding import PartitionSpec as P

R = 32
LANES = 128
CORES = 2
COARSE_FACTOR = 0.5
EARLY = 144
VMEM_LIMIT = 48 << 20


def widen(source, target, block):
    def step(i, carry):
        first = pl.multiple_of(i * block, block)
        target[pl.ds(first, block), :] = source[pl.ds(first, block), :].astype(jnp.float32)
        return carry

    lax.fori_loop(0, source.shape[0] // block, step, 0)


def gather_rows(lists, table, out, first, count, unroll):
    def step(i, carry):
        for k in range(unroll):
            r = i * unroll + k
            picked = [table[pl.ds(entries[0, first + r], 1), :] for entries in lists]
            for s, row in enumerate(picked):
                out[s, pl.ds(r, 1), :] = row
        return carry

    lax.fori_loop(0, count // unroll, step, 0)


def pick_kernel(wanted_ref, own_ref, out_ref, table, rows, sem, *lists):
    copies = [pltpu.make_async_copy(wanted_ref.at[s], entries, sem) for s, entries in enumerate(lists)]
    for copy in copies:
        copy.start()
    count = own_ref.shape[0]
    widen(own_ref, table, 128)
    table[pl.ds(count, 8), :] = jnp.zeros((8, LANES), jnp.float32)
    for copy in copies:
        copy.wait()
    gather_rows(lists, table, rows, 0, rows.shape[1], 2)

    def narrow(s, carry):
        out_ref[s] = rows[s].astype(out_ref.dtype)
        return carry

    lax.fori_loop(0, len(lists), narrow, 0)


def pick(own, wanted):
    parts, _, length = wanted.shape
    vmem = pl.BlockSpec(memory_space=pltpu.VMEM)
    return pl.pallas_call(
        pick_kernel,
        out_shape=jax.ShapeDtypeStruct((parts, length, LANES), own.dtype),
        in_specs=[pl.BlockSpec(memory_space=pl.ANY), vmem],
        out_specs=vmem,
        scratch_shapes=[
            pltpu.VMEM((own.shape[0] + 8, LANES), jnp.float32),
            pltpu.VMEM((parts, length, LANES), jnp.float32),
            pltpu.SemaphoreType.DMA,
        ]
        + [pltpu.SMEM((1, length), jnp.int32)] * parts,
        compiler_params=pltpu.CompilerParams(vmem_limit_bytes=VMEM_LIMIT),
        cost_estimate=pl.CostEstimate(
            flops=0, bytes_accessed=2 * parts * length * LANES * 8, transcendentals=0
        ),
        name="pick",
    )(wanted, own)


def operator_sum(rows, weights, count):
    operators, _, columns = weights.shape
    total = jnp.zeros((count, columns), jnp.float32)
    together = 8
    for first in range(0, operators, together):
        left = jnp.concatenate(
            [rows[first + o, pl.ds(0, count), :].astype(jnp.bfloat16) for o in range(together)],
            axis=1,
        )
        right = weights[pl.ds(first, together)].reshape(together * LANES, columns)
        total = total + jnp.dot(left, right, preferred_element_type=jnp.float32)
    return total


def translate_kernel(jobs, halo, idx_ref, at_ref, own_ref, got_ref, ops_ref, *refs):
    weight_refs, refs = refs[:6], refs[6:]
    outs, refs = refs[: len(jobs)], refs[len(jobs) :]
    table, landed, rows, weights, got_sem, list_sem, weight_sem = refs[:7]
    lists = refs[7:]
    operators = rows.shape[0]
    members, ops = 4, ops_ref.shape[0]
    me, core = at_ref[0], at_ref[1]
    own, got = own_ref.shape[0], landed.shape[0]
    piece = got // got_sem.shape[0]
    arrivals = []
    for n in range(got // piece):
        part = pl.ds(n * piece, piece)
        arrivals.append(
            pltpu.make_async_copy(got_ref.at[part, :], landed.at[part, :], got_sem.at[n])
        )
    stride = (idx_ref.shape[2] - LANES) // members
    sets = [
        (pl.multiple_of(lax.rem(me + shift, members) * stride, LANES), first, count)
        for shift, first, count in jobs
    ]
    if halo:
        sets = [(members * stride, 0, halo)] + sets
    copies = []
    for n, (start, _, _) in enumerate(sets):
        batch = []
        for o in range(operators):
            entries = lists[n * operators + o]
            source = idx_ref.at[o, :, pl.ds(start, entries.shape[1])]
            batch.append(pltpu.make_async_copy(source, entries, list_sem.at[n]))
        copies.append(batch)
    columns = pl.ds(pl.multiple_of(me * LANES, LANES), LANES)
    heavy = [
        pltpu.make_async_copy(ops_ref.at[:, columns, :], weights.at[pl.ds(0, ops)], weight_sem)
    ]
    half = ops // 2
    for n, ref in enumerate(weight_refs):
        side = core if n % 2 == 0 else 1 - core
        place = weights.at[pl.ds((n // 2 + 1) * ops + side * half, half)]
        heavy.append(pltpu.make_async_copy(ref, place, weight_sem))
    for copy in arrivals + copies[0] + heavy:
        copy.start()
    for batch in copies[1:]:
        for copy in batch:
            copy.start()
    widen(own_ref, table, 128)
    table[pl.ds(own + got, 8), :] = jnp.zeros((8, LANES), jnp.float32)
    for n, copy in enumerate(arrivals):
        copy.wait()
        widen(
            landed.at[pl.ds(n * piece, piece), :], table.at[pl.ds(own + n * piece, piece), :], 512
        )
    for n, (_, first, count) in enumerate(sets):
        for copy in copies[n]:
            copy.wait()
        chosen = lists[n * operators : (n + 1) * operators]
        gather_rows(chosen, table, rows, first, count, 8)
        if n == 0:
            for copy in heavy:
                copy.wait()
        total = operator_sum(rows, weights, count)
        if halo and n == 0:
            for out in outs:
                out[pl.ds(out.shape[0] - halo, halo), :] = total.astype(out.dtype)
        else:
            out = outs[n - (1 if halo else 0)]
            out[pl.ds(0, count), :] = total.astype(out.dtype)


def translate(idx, at, own, got, operators, weights, jobs, halo, dtypes):
    every, columns = idx.shape[0], operators.shape[2]
    vmem = pl.BlockSpec(memory_space=pltpu.VMEM)
    hbm = pl.BlockSpec(memory_space=pltpu.HBM)
    stride = (idx.shape[2] - LANES) // 4
    lengths = ([LANES] if halo else []) + [stride] * len(jobs)
    counts = [count for _, _, count in jobs]
    return pl.pallas_call(
        functools.partial(translate_kernel, jobs, halo),
        out_shape=[
            jax.ShapeDtypeStruct((count + halo, columns), dtype)
            for count, dtype in zip(counts, dtypes)
        ],
        in_specs=[hbm, pl.BlockSpec(memory_space=pltpu.SMEM), vmem] + [hbm] * (2 + len(weights)),
        out_specs=[vmem] * len(jobs),
        scratch_shapes=[
            pltpu.VMEM((own.shape[0] + got.shape[0] + 8, LANES), jnp.float32),
            pltpu.VMEM(got.shape, own.dtype),
            pltpu.VMEM((every, max(counts), LANES), jnp.float32),
            pltpu.VMEM((every, LANES, columns), operators.dtype),
            pltpu.SemaphoreType.DMA((4,)),
            pltpu.SemaphoreType.DMA((len(lengths),)),
            pltpu.SemaphoreType.DMA,
        ]
        + [pltpu.SMEM((1, length), jnp.int32) for length in lengths for _ in range(every)],
        compiler_params=pltpu.CompilerParams(vmem_limit_bytes=VMEM_LIMIT),
        cost_estimate=pl.CostEstimate(
            flops=2 * every * LANES * columns * sum(counts),
            bytes_accessed=2 * every * (sum(counts) + halo) * LANES * 8,
            transcendentals=0,
        ),
        name="translate",
    )(idx, at, own, got, operators, *weights)


def edge_kernel(own_ref, a_ref, b_ref, c_ref, head_ref, tail_ref):
    half = head_ref.shape[0]
    for out, last in ((head_ref, 2 * half), (tail_ref, half)):
        total = jnp.zeros(out.shape, jnp.float32)
        for ref in (own_ref, a_ref, b_ref, c_ref):
            total = total + ref[pl.ds(ref.shape[0] - last, half), :].astype(jnp.float32)
        out[...] = total.astype(out.dtype)


def edges(parts, halo):
    half = jax.ShapeDtypeStruct((halo // 2, parts[0].shape[1]), parts[0].dtype)
    vmem = pl.BlockSpec(memory_space=pltpu.VMEM)
    return pl.pallas_call(
        edge_kernel,
        out_shape=[half, half],
        in_specs=[vmem] * 4,
        out_specs=[vmem] * 2,
        compiler_params=pltpu.CompilerParams(vmem_limit_bytes=VMEM_LIMIT),
        name="edges",
    )(*parts)


def finish_kernel(
    own_ref, a_ref, b_ref, early_ref, late_ref, place_ref, left_ref, right_ref, l2l_ref, out_ref, acc
):
    rows, columns = out_ref.shape
    octants = l2l_ref.shape[0]
    count = rows // octants
    split = own_ref.shape[0] - late_ref.shape[0]

    def total(first, size):
        part = own_ref[pl.ds(first, size), :]
        for ref in (a_ref, b_ref):
            part = part + ref[pl.ds(first, size), :].astype(jnp.float32)
        head = [early_ref[pl.ds(first, split - first), :]] if first < split else []
        tail = late_ref[pl.ds(max(first - split, 0), size - max(split - first, 0)), :]
        return part + jnp.concatenate(head + [tail], axis=0).astype(jnp.float32)

    parent = (total(rows, count) * COARSE_FACTOR).astype(jnp.bfloat16)
    slabs = columns // LANES
    for k in range(octants):
        child = jnp.dot(parent, l2l_ref[k], preferred_element_type=jnp.float32)
        for j in range(slabs):
            acc[j, pl.ds(k, count, stride=octants), :] = child[:, j * LANES : (j + 1) * LANES]
    fine = total(0, rows).astype(jnp.bfloat16).astype(jnp.float32)
    halo = jnp.concatenate([left_ref[...], right_ref[...]], axis=0)
    spread = (
        lax.broadcasted_iota(jnp.int32, (halo.shape[0], rows), 0) == place_ref[...]
    ).astype(jnp.bfloat16)
    foreign = lax.dot_general(
        spread, halo, (((0,), (0,)), ((), ())), preferred_element_type=jnp.float32
    )
    far = fine + foreign
    for j in range(slabs):
        lanes = slice(j * LANES, (j + 1) * LANES)
        out_ref[:, lanes] = (acc[j] + far[:, lanes]).astype(out_ref.dtype)


def finish(own, parts, place, left, right, l2l_ops):
    rows, columns = place.shape[1], own.shape[1]
    vmem = pl.BlockSpec(memory_space=pltpu.VMEM)
    return pl.pallas_call(
        finish_kernel,
        out_shape=jax.ShapeDtypeStruct((rows, columns), jnp.bfloat16),
        in_specs=[vmem] * 9,
        out_specs=vmem,
        scratch_shapes=[pltpu.VMEM((columns // LANES, rows, LANES), jnp.float32)],
        compiler_params=pltpu.CompilerParams(vmem_limit_bytes=VMEM_LIMIT),
        name="finish",
    )(own, *parts, place, left, right, l2l_ops)


def per_device(
    exp_fine, req_fine, src_fine, exp_coarse, req_coarse, src_coarse, operators, l2l_ops, relay_src
):
    members = lax.axis_size("grp")
    me = lax.axis_index("grp")
    blocks = lax.axis_size("box")
    here = lax.axis_index("box")
    rows_f, rows_c = exp_fine.shape[0], exp_coarse.shape[0]
    slots_f, slots_c = req_fine.shape[1], req_coarse.shape[1]
    own_rows, slots = rows_f + rows_c, slots_f + slots_c
    zero_row = own_rows + blocks * slots
    ops, coefficients, _ = operators.shape
    quarter_f, quarter_c = rows_f // members, rows_c // members
    chunk = quarter_f + quarter_c
    at = jnp.stack([me, here % CORES]).astype(jnp.int32)

    def shifted(value, by):
        return lax.ppermute(value, "grp", [(i, (i + by) % members) for i in range(members)])

    def swapped(value):
        return lax.ppermute(value, "box", [(i, i ^ 1) for i in range(blocks)])

    asked = jnp.concatenate([req_fine, req_coarse], axis=1)[:, None, :]
    starts = jnp.where(jnp.arange(slots) < slots_f, 0, rows_f)
    requests = jnp.where(asked >= 0, asked + starts, own_rows)
    wanted = lax.all_to_all(requests, "box", split_axis=0, concat_axis=0, tiled=True)
    own = jnp.concatenate(
        [
            lax.dynamic_slice_in_dim(exp_fine, me * LANES, LANES, 1),
            lax.dynamic_slice_in_dim(exp_coarse, me * LANES, LANES, 1),
        ],
        axis=0,
    )
    sent = pick(own, wanted)
    got = lax.all_to_all(sent, "box", split_axis=0, concat_axis=0, tiled=True)
    got = got.reshape(blocks * slots, LANES)

    raw = jnp.concatenate([src_fine, src_coarse], axis=1)
    raws = [raw] + [shifted(raw, s) for s in range(1, members)]
    raws, held = lax.optimization_barrier((raws, operators))
    raw = jnp.concatenate(raws, axis=0)

    half = ops // CORES
    weights = []
    for s in range(1, members):
        start = ((here % CORES) * half, ((me + s) % members) * LANES, 0)
        fetched = shifted(lax.dynamic_slice(held, start, (half, LANES, coefficients)), s)
        weights += [fetched, swapped(fetched)]

    src_f, src_c = raw[:, :rows_f], raw[:, rows_f:]
    q = src_f - rows_f
    table_f = jnp.where(src_f < rows_f, src_f, own_rows + (q // slots_f) * slots + q % slots_f)
    table_f = jnp.where(src_f >= 0, table_f, zero_row)
    q = src_c - rows_c
    table_c = own_rows + (q // slots_c) * slots + slots_f + q % slots_c
    table_c = jnp.where(src_c < rows_c, src_c + rows_f, table_c)
    table_c = jnp.where(src_c >= 0, table_c, zero_row)
    local = relay_src - here * rows_f
    inside = (local >= 0) & (local < rows_f)
    relayed = jnp.take(table_f.T, jnp.clip(local, 0, rows_f - 1), axis=0).T
    relayed = jnp.where(inside[None, :], relayed, zero_row)
    every = members * ops
    gap = -chunk % LANES
    chunks = jnp.concatenate(
        [
            relayed.reshape(every, members, quarter_f),
            table_c.reshape(every, members, quarter_c),
            jnp.full((every, members, gap), zero_row, jnp.int32),
        ],
        axis=2,
    )
    idx = jnp.concatenate(
        [
            chunks.reshape(every, -1),
            table_f[:, :R],
            table_f[:, rows_f - R :],
            jnp.full((every, LANES - 2 * R), zero_row, jnp.int32),
        ],
        axis=1,
    )[:, None, :]
    place = jnp.where(local < 0, local + R, jnp.where(local >= rows_f, local - rows_f + R, -1))
    place = lax.dynamic_slice_in_dim(place, me * quarter_f, quarter_f, 0)[None, :]
    got, place, idx = lax.optimization_barrier((got, place, idx))

    def sums(jobs, halo, dtypes):
        return translate(idx, at, own, got, operators, weights, jobs, halo, dtypes)

    narrow = jnp.bfloat16
    whole = (0, chunk)
    away = sums(((2, *whole), (1, *whole), (3, 0, EARLY)), 2 * R, (narrow, narrow, narrow))
    others = [shifted(part, s) for part, s in zip(away, (2, 1, 3))]
    late, mine = sums(((3, EARLY, chunk - EARLY), (0, *whole)), 0, (narrow, jnp.float32))
    others, late, mine = lax.optimization_barrier((others, late, mine))
    head, tail = edges([away[0]] + others, 2 * R)
    from_left = lax.ppermute(tail, "box", [(i, i + 1) for i in range(blocks - 1)])
    from_right = lax.ppermute(head, "box", [(i + 1, i) for i in range(blocks - 1)])
    others = others + [shifted(late, 3)]
    done = finish(mine, others, place, from_left, from_right, l2l_ops)
    out = jnp.zeros((rows_f, coefficients), jnp.bfloat16)
    for s in (0, 2, 1, 3):
        piece = done if s == 0 else shifted(done, s)
        out = lax.dynamic_update_slice_in_dim(out, piece, ((me - s) % members) * quarter_f, 0)
    return out


def solution(mesh):
    return jax.shard_map(
        per_device,
        mesh=mesh,
        in_specs=(
            P("box", None),
            P("box", None),
            P(("box", "grp"), None),
            P("box", None),
            P("box", None),
            P(("box", "grp"), None),
            P("grp", None, None),
            P(),
            P("box"),
        ),
        out_specs=P("box", None),
        check_vma=False,
    )
```

```python
import functools

import jax
import jax.numpy as jnp
from jax import lax
from jax.experimental import pallas as pl
from jax.experimental.pallas import tpu as pltpu
from jax.sharding import PartitionSpec as P

R = 32
LANES = 128
CORES = 2
COARSE_FACTOR = 0.5
EARLY = 144
VMEM_LIMIT = 48 << 20


def widen(source, target, block):
    def step(i, carry):
        first = pl.multiple_of(i * block, block)
        target[pl.ds(first, block), :] = source[pl.ds(first, block), :].astype(jnp.float32)
        return carry

    lax.fori_loop(0, source.shape[0] // block, step, 0)


def gather_rows(lists, table, out, first, count, unroll):
    def step(i, carry):
        for k in range(unroll):
            r = i * unroll + k
            picked = [table[pl.ds(entries[0, first + r], 1), :] for entries in lists]
            for s, row in enumerate(picked):
                out[s, pl.ds(r, 1), :] = row
        return carry

    lax.fori_loop(0, count // unroll, step, 0)


def pick_kernel(wanted_ref, own_ref, out_ref, table, rows, sem, *lists):
    copies = [pltpu.make_async_copy(wanted_ref.at[s], entries, sem) for s, entries in enumerate(lists)]
    for copy in copies:
        copy.start()
    count = own_ref.shape[0]
    widen(own_ref, table, 128)
    table[pl.ds(count, 8), :] = jnp.zeros((8, LANES), jnp.float32)
    for copy in copies:
        copy.wait()
    gather_rows(lists, table, rows, 0, rows.shape[1], 2)

    def narrow(s, carry):
        out_ref[s] = rows[s].astype(out_ref.dtype)
        return carry

    lax.fori_loop(0, len(lists), narrow, 0)


def pick(own, wanted):
    parts, _, length = wanted.shape
    vmem = pl.BlockSpec(memory_space=pltpu.VMEM)
    return pl.pallas_call(
        pick_kernel,
        out_shape=jax.ShapeDtypeStruct((parts, length, LANES), own.dtype),
        in_specs=[pl.BlockSpec(memory_space=pl.ANY), vmem],
        out_specs=vmem,
        scratch_shapes=[
            pltpu.VMEM((own.shape[0] + 8, LANES), jnp.float32),
            pltpu.VMEM((parts, length, LANES), jnp.float32),
            pltpu.SemaphoreType.DMA,
        ]
        + [pltpu.SMEM((1, length), jnp.int32)] * parts,
        compiler_params=pltpu.CompilerParams(vmem_limit_bytes=VMEM_LIMIT),
        cost_estimate=pl.CostEstimate(
            flops=0, bytes_accessed=2 * parts * length * LANES * 8, transcendentals=0
        ),
        name="pick",
    )(wanted, own)


def operator_sum(rows, weights, count):
    operators, _, columns = weights.shape
    total = jnp.zeros((count, columns), jnp.float32)
    together = 8
    for first in range(0, operators, together):
        left = jnp.concatenate(
            [rows[first + o, pl.ds(0, count), :].astype(jnp.bfloat16) for o in range(together)],
            axis=1,
        )
        right = weights[pl.ds(first, together)].reshape(together * LANES, columns)
        total = total + jnp.dot(left, right, preferred_element_type=jnp.float32)
    return total


def translate_kernel(jobs, halo, idx_ref, at_ref, own_ref, got_ref, ops_ref, *refs):
    weight_refs, refs = refs[:6], refs[6:]
    outs, refs = refs[: len(jobs)], refs[len(jobs) :]
    table, landed, rows, weights, got_sem, list_sem, weight_sem = refs[:7]
    lists = refs[7:]
    operators = rows.shape[0]
    members, ops = 4, ops_ref.shape[0]
    me, core = at_ref[0], at_ref[1]
    own, got = own_ref.shape[0], landed.shape[0]
    piece = got // got_sem.shape[0]
    arrivals = []
    for n in range(got // piece):
        part = pl.ds(n * piece, piece)
        arrivals.append(
            pltpu.make_async_copy(got_ref.at[part, :], landed.at[part, :], got_sem.at[n])
        )
    stride = (idx_ref.shape[2] - LANES) // members
    sets = [
        (pl.multiple_of(lax.rem(me + shift, members) * stride, LANES), first, count)
        for shift, first, count in jobs
    ]
    if halo:
        sets = [(members * stride, 0, halo)] + sets
    copies = []
    for n, (start, _, _) in enumerate(sets):
        batch = []
        for o in range(operators):
            entries = lists[n * operators + o]
            source = idx_ref.at[o, :, pl.ds(start, entries.shape[1])]
            batch.append(pltpu.make_async_copy(source, entries, list_sem.at[n]))
        copies.append(batch)
    columns = pl.ds(pl.multiple_of(me * LANES, LANES), LANES)
    heavy = [
        pltpu.make_async_copy(ops_ref.at[:, columns, :], weights.at[pl.ds(0, ops)], weight_sem)
    ]
    half = ops // 2
    for n, ref in enumerate(weight_refs):
        side = core if n % 2 == 0 else 1 - core
        place = weights.at[pl.ds((n // 2 + 1) * ops + side * half, half)]
        heavy.append(pltpu.make_async_copy(ref, place, weight_sem))
    for copy in arrivals + copies[0] + heavy:
        copy.start()
    for batch in copies[1:]:
        for copy in batch:
            copy.start()
    widen(own_ref, table, 128)
    table[pl.ds(own + got, 8), :] = jnp.zeros((8, LANES), jnp.float32)
    for n, copy in enumerate(arrivals):
        copy.wait()
        widen(
            landed.at[pl.ds(n * piece, piece), :], table.at[pl.ds(own + n * piece, piece), :], 512
        )
    for n, (_, first, count) in enumerate(sets):
        for copy in copies[n]:
            copy.wait()
        chosen = lists[n * operators : (n + 1) * operators]
        gather_rows(chosen, table, rows, first, count, 8)
        if n == 0:
            for copy in heavy:
                copy.wait()
        total = operator_sum(rows, weights, count)
        if halo and n == 0:
            for out in outs:
                out[pl.ds(out.shape[0] - halo, halo), :] = total.astype(out.dtype)
        else:
            out = outs[n - (1 if halo else 0)]
            out[pl.ds(0, count), :] = total.astype(out.dtype)


def translate(idx, at, own, got, operators, weights, jobs, halo, dtypes):
    every, columns = idx.shape[0], operators.shape[2]
    vmem = pl.BlockSpec(memory_space=pltpu.VMEM)
    hbm = pl.BlockSpec(memory_space=pltpu.HBM)
    stride = (idx.shape[2] - LANES) // 4
    lengths = ([LANES] if halo else []) + [stride] * len(jobs)
    counts = [count for _, _, count in jobs]
    return pl.pallas_call(
        functools.partial(translate_kernel, jobs, halo),
        out_shape=[
            jax.ShapeDtypeStruct((count + halo, columns), dtype)
            for count, dtype in zip(counts, dtypes)
        ],
        in_specs=[hbm, pl.BlockSpec(memory_space=pltpu.SMEM), vmem] + [hbm] * (2 + len(weights)),
        out_specs=[vmem] * len(jobs),
        scratch_shapes=[
            pltpu.VMEM((own.shape[0] + got.shape[0] + 8, LANES), jnp.float32),
            pltpu.VMEM(got.shape, own.dtype),
            pltpu.VMEM((every, max(counts), LANES), jnp.float32),
            pltpu.VMEM((every, LANES, columns), operators.dtype),
            pltpu.SemaphoreType.DMA((4,)),
            pltpu.SemaphoreType.DMA((len(lengths),)),
            pltpu.SemaphoreType.DMA,
        ]
        + [pltpu.SMEM((1, length), jnp.int32) for length in lengths for _ in range(every)],
        compiler_params=pltpu.CompilerParams(vmem_limit_bytes=VMEM_LIMIT),
        cost_estimate=pl.CostEstimate(
            flops=2 * every * LANES * columns * sum(counts),
            bytes_accessed=2 * every * (sum(counts) + halo) * LANES * 8,
            transcendentals=0,
        ),
        name="translate",
    )(idx, at, own, got, operators, *weights)


def edge_kernel(own_ref, a_ref, b_ref, c_ref, head_ref, tail_ref):
    half = head_ref.shape[0]
    for out, last in ((head_ref, 2 * half), (tail_ref, half)):
        total = jnp.zeros(out.shape, jnp.float32)
        for ref in (own_ref, a_ref, b_ref, c_ref):
            total = total + ref[pl.ds(ref.shape[0] - last, half), :].astype(jnp.float32)
        out[...] = total.astype(out.dtype)


def edges(parts, halo):
    half = jax.ShapeDtypeStruct((halo // 2, parts[0].shape[1]), parts[0].dtype)
    vmem = pl.BlockSpec(memory_space=pltpu.VMEM)
    return pl.pallas_call(
        edge_kernel,
        out_shape=[half, half],
        in_specs=[vmem] * 4,
        out_specs=[vmem] * 2,
        compiler_params=pltpu.CompilerParams(vmem_limit_bytes=VMEM_LIMIT),
        name="edges",
    )(*parts)


def finish_kernel(
    own_ref, a_ref, b_ref, early_ref, late_ref, place_ref, left_ref, right_ref, l2l_ref, out_ref, acc
):
    rows, columns = out_ref.shape
    octants = l2l_ref.shape[0]
    count = rows // octants
    split = own_ref.shape[0] - late_ref.shape[0]

    def total(first, size):
        part = own_ref[pl.ds(first, size), :]
        for ref in (a_ref, b_ref):
            part = part + ref[pl.ds(first, size), :].astype(jnp.float32)
        head = [early_ref[pl.ds(first, split - first), :]] if first < split else []
        tail = late_ref[pl.ds(max(first - split, 0), size - max(split - first, 0)), :]
        return part + jnp.concatenate(head + [tail], axis=0).astype(jnp.float32)

    parent = (total(rows, count) * COARSE_FACTOR).astype(jnp.bfloat16)
    slabs = columns // LANES
    for k in range(octants):
        child = jnp.dot(parent, l2l_ref[k], preferred_element_type=jnp.float32)
        for j in range(slabs):
            acc[j, pl.ds(k, count, stride=octants), :] = child[:, j * LANES : (j + 1) * LANES]
    fine = total(0, rows).astype(jnp.bfloat16).astype(jnp.float32)
    halo = jnp.concatenate([left_ref[...], right_ref[...]], axis=0)
    spread = (
        lax.broadcasted_iota(jnp.int32, (halo.shape[0], rows), 0) == place_ref[...]
    ).astype(jnp.bfloat16)
    foreign = lax.dot_general(
        spread, halo, (((0,), (0,)), ((), ())), preferred_element_type=jnp.float32
    )
    far = fine + foreign
    for j in range(slabs):
        lanes = slice(j * LANES, (j + 1) * LANES)
        out_ref[:, lanes] = (acc[j] + far[:, lanes]).astype(out_ref.dtype)


def finish(own, parts, place, left, right, l2l_ops):
    rows, columns = place.shape[1], own.shape[1]
    vmem = pl.BlockSpec(memory_space=pltpu.VMEM)
    return pl.pallas_call(
        finish_kernel,
        out_shape=jax.ShapeDtypeStruct((rows, columns), jnp.bfloat16),
        in_specs=[vmem] * 9,
        out_specs=vmem,
        scratch_shapes=[pltpu.VMEM((columns // LANES, rows, LANES), jnp.float32)],
        compiler_params=pltpu.CompilerParams(vmem_limit_bytes=VMEM_LIMIT),
        name="finish",
    )(own, *parts, place, left, right, l2l_ops)


def per_device(
    exp_fine, req_fine, src_fine, exp_coarse, req_coarse, src_coarse, operators, l2l_ops, relay_src
):
    members = lax.axis_size("grp")
    me = lax.axis_index("grp")
    blocks = lax.axis_size("box")
    here = lax.axis_index("box")
    rows_f, rows_c = exp_fine.shape[0], exp_coarse.shape[0]
    slots_f, slots_c = req_fine.shape[1], req_coarse.shape[1]
    own_rows, slots = rows_f + rows_c, slots_f + slots_c
    zero_row = own_rows + blocks * slots
    ops, coefficients, _ = operators.shape
    quarter_f, quarter_c = rows_f // members, rows_c // members
    chunk = quarter_f + quarter_c
    at = jnp.stack([me, here % CORES]).astype(jnp.int32)

    def shifted(value, by):
        return lax.ppermute(value, "grp", [(i, (i + by) % members) for i in range(members)])

    def swapped(value):
        return lax.ppermute(value, "box", [(i, i ^ 1) for i in range(blocks)])

    asked = jnp.concatenate([req_fine, req_coarse], axis=1)[:, None, :]
    starts = jnp.where(jnp.arange(slots) < slots_f, 0, rows_f)
    requests = jnp.where(asked >= 0, asked + starts, own_rows)
    wanted = lax.all_to_all(requests, "box", split_axis=0, concat_axis=0, tiled=True)
    own = jnp.concatenate(
        [
            lax.dynamic_slice_in_dim(exp_fine, me * LANES, LANES, 1),
            lax.dynamic_slice_in_dim(exp_coarse, me * LANES, LANES, 1),
        ],
        axis=0,
    )
    sent = pick(own, wanted)
    got = lax.all_to_all(sent, "box", split_axis=0, concat_axis=0, tiled=True)
    got = got.reshape(blocks * slots, LANES)

    raw = jnp.concatenate([src_fine, src_coarse], axis=1)
    raws = [raw] + [shifted(raw, s) for s in range(1, members)]
    raws, held = lax.optimization_barrier((raws, operators))
    raw = jnp.concatenate(raws, axis=0)

    half = ops // CORES
    weights = []
    for s in range(1, members):
        start = ((here % CORES) * half, ((me + s) % members) * LANES, 0)
        fetched = shifted(lax.dynamic_slice(held, start, (half, LANES, coefficients)), s)
        weights += [fetched, swapped(fetched)]

    src_f, src_c = raw[:, :rows_f], raw[:, rows_f:]
    q = src_f - rows_f
    table_f = jnp.where(src_f < rows_f, src_f, own_rows + (q // slots_f) * slots + q % slots_f)
    table_f = jnp.where(src_f >= 0, table_f, zero_row)
    q = src_c - rows_c
    table_c = own_rows + (q // slots_c) * slots + slots_f + q % slots_c
    table_c = jnp.where(src_c < rows_c, src_c + rows_f, table_c)
    table_c = jnp.where(src_c >= 0, table_c, zero_row)
    local = relay_src - here * rows_f
    inside = (local >= 0) & (local < rows_f)
    relayed = jnp.take(table_f.T, jnp.clip(local, 0, rows_f - 1), axis=0).T
    relayed = jnp.where(inside[None, :], relayed, zero_row)
    every = members * ops
    gap = -chunk % LANES
    chunks = jnp.concatenate(
        [
            relayed.reshape(every, members, quarter_f),
            table_c.reshape(every, members, quarter_c),
            jnp.full((every, members, gap), zero_row, jnp.int32),
        ],
        axis=2,
    )
    idx = jnp.concatenate(
        [
            chunks.reshape(every, -1),
            table_f[:, :R],
            table_f[:, rows_f - R :],
            jnp.full((every, LANES - 2 * R), zero_row, jnp.int32),
        ],
        axis=1,
    )[:, None, :]
    place = jnp.where(local < 0, local + R, jnp.where(local >= rows_f, local - rows_f + R, -1))
    place = lax.dynamic_slice_in_dim(place, me * quarter_f, quarter_f, 0)[None, :]
    got, place, idx = lax.optimization_barrier((got, place, idx))

    def sums(jobs, halo, dtypes):
        return translate(idx, at, own, got, operators, weights, jobs, halo, dtypes)

    narrow = jnp.bfloat16
    whole = (0, chunk)
    away = sums(((2, *whole), (1, *whole), (3, 0, EARLY)), 2 * R, (narrow, narrow, narrow))
    others = [shifted(part, s) for part, s in zip(away, (2, 1, 3))]
    late, mine = sums(((3, EARLY, chunk - EARLY), (0, *whole)), 0, (narrow, jnp.float32))
    others, late, mine = lax.optimization_barrier((others, late, mine))
    head, tail = edges([away[0]] + others, 2 * R)
    from_left = lax.ppermute(tail, "box", [(i, i + 1) for i in range(blocks - 1)])
    from_right = lax.ppermute(head, "box", [(i + 1, i) for i in range(blocks - 1)])
    late, from_left = lax.optimization_barrier((late, from_left))
    others = others + [shifted(late, 3)]
    done = finish(mine, others, place, from_left, from_right, l2l_ops)
    out = jnp.zeros((rows_f, coefficients), jnp.bfloat16)
    for s in (0, 2, 1, 3):
        piece = done if s == 0 else shifted(done, s)
        out = lax.dynamic_update_slice_in_dim(out, piece, ((me - s) % members) * quarter_f, 0)
    return out


def solution(mesh):
    return jax.shard_map(
        per_device,
        mesh=mesh,
        in_specs=(
            P("box", None),
            P("box", None),
            P(("box", "grp"), None),
            P("box", None),
            P("box", None),
            P(("box", "grp"), None),
            P("grp", None, None),
            P(),
            P("box"),
        ),
        out_specs=P("box", None),
        check_vma=False,
    )
```
